128 devices in a mesh: gx: 8 (over z_lo, x), gy: 16 (over z_hi, y, core).
Axes of the slice: x: 4, y: 4, z: 4 (z_hi: 2, z_lo: 2; z = z_hi * 2 + z_lo), core: 2. Of those that a mesh axis runs over, the one named last changes fastest.
Arguments:
- velocity: float32 [3, 256, 1024, 128], P(None, 'gx', 'gy'), may hold values from -6 to 6
- stress: float32 [6, 256, 1024, 128], P(None, 'gx', 'gy'), may hold values from -6 to 6
- region_id: int32 [256, 1024, 128], P('gx', 'gy'), may hold values from 0 to 15
- buoyancy: float32 [16], replicated, may hold values from 0.5 to 1
- lame_lambda: float32 [16], replicated, may hold values from 0.5 to 2
- shear_mu: float32 [16], replicated, may hold values from 0.25 to 1
- shell_rows: float32 [32768, 9, 128], P(('gx', 'gy')), may hold values from -6 to 6
- shell_target: int32 [32768, 1], P(('gx', 'gy')), may hold values from 0 to 127; in each aligned block of 256 rows (0 to 255, 256 to 511, ...) at most 4 rows name the same one
- shell_cell: int32 [32768, 1], P(('gx', 'gy')), may hold values from 0 to 2047
- pile_pier: int32 [32768, 1], P(('gx', 'gy')), may hold values from 0 to 127; in each aligned block of 256 rows (0 to 255, 256 to 511, ...) at most 4 rows name the same one
- pile_cell: int32 [32768, 1], P(('gx', 'gy')), may hold values from 0 to 2047
- pier_owner: int32 [128], replicated, may hold values from 0 to 127, each once
Outputs:
- velocity_out: float32 [3, 256, 1024, 128], P(None, 'gx', 'gy')
- stress_out: float32 [6, 256, 1024, 128], P(None, 'gx', 'gy')
- pier_force: float32 [128, 384], P(('gx', 'gy'))
The draws below stay inside these ranges and needn't reach their ends.
Inputs may be any that keep to these rules, and one draw needn't show every extreme that they name: `shell_target`: within the rows of one device (aligned blocks of 256 rows), no device number appears more than 4 times, and some number appears exactly 4 times. `shell_cell`: A column number inside the target device's block. `pile_pier`: within the rows of one device (aligned blocks of 256 rows), no pier appears more than 4 times, and some pier appears exactly 4 times. `pile_cell`: A column number inside the block of the device that lists the pile. `pier_owner`: A permutation; the pier with owner slot s is owned by device s.
All inputs are finite; a program needn't handle non-finite values.
Results may differ from the reference program's by a relative error of at most 0.00002.
Values sent between devices are 32-bit elements; how exact they have to be, the bound alone decides.
A program may use at most 192 MiB of HBM per device.

```python
import math
import jax
import jax.numpy as jnp
import numpy as np

NZ = 128
CX = 32
CY = 64
REGIONS = 16
PML = 8
SH_DEV = 256
PIER_DEV = 1
PILE_DEV = 256
NX = 256
NY = 1024
SHELL = 32768
CAP = 4
PIERS = 128
PILES = 32768
CAPP = 4
N_GY = 16
DEVICES = 128


def with_ends(result, own_key, least, top_value):
    longest = result.shape.index(max(result.shape))
    spots = []
    for shift in (0, 1):
        where = [jax.random.randint(jax.random.fold_in(own_key, axis), (), 0, length) for axis, length in enumerate(result.shape)]
        where[longest] = (where[longest] + shift) % result.shape[longest]
        spots.append(tuple(where))
    return result.at[spots[0]].set(least).at[spots[1]].set(top_value)


def shard_levels(own_key, dims, shards, least, high):
    gain = 1.0
    for axis_at, blocks in shards:
        draws = jax.random.uniform(jax.random.fold_in(jax.random.fold_in(own_key, 6), axis_at), (blocks,), jnp.float32, least / len(shards), high / len(shards))
        gain = gain * jnp.repeat(jnp.exp(draws), dims[axis_at] // blocks).reshape((-1,) + (1,) * (len(dims) - 1 - axis_at))
    return gain


def assign_block(stream_key, own, number, rows, count, top, bound, skew):
    order = jax.random.permutation(stream_key, count)
    crowded, ordinary = load_shares(count, rows * top, bound, skew, True), load_shares(count, rows * top, bound, skew, False)
    places = jnp.arange(count)

    def named(tallies, rotation):
        used = int((tallies > 0).sum())
        fixed = max(1, used // 4)
        passed = fixed + (places - fixed + rotation * (used - fixed)) % max(1, count - fixed)
        return jnp.zeros((count,), jnp.int32).at[order[jnp.where(places < fixed, places, passed)]].set(jnp.asarray(tallies, jnp.int32))

    tallies = jnp.where(number % 4 == 0, named(crowded, number // 4), named(ordinary, number - number // 4 - 1))
    mixed = jax.random.permutation(jax.random.fold_in(own, 3), count)
    giver, taker = mixed[0:count // 2 * 2:2], mixed[1:count // 2 * 2:2]
    margin = jnp.minimum(tallies[giver] - 1, bound - tallies[taker]) // 2
    margin = jnp.where((giver == order[0]) | (taker == order[0]) | (tallies[taker] == 0), 0, jnp.maximum(margin, 0))
    passed = jax.random.randint(jax.random.fold_in(own, 4), (count // 2,), 0, 1 << 20) % (margin + 1)
    tallies = tallies.at[giver].add(-passed).at[taker].add(passed)
    members = jnp.searchsorted(jnp.cumsum(tallies), jnp.arange(rows * top), side="right").astype(jnp.int32)
    listing = members.reshape(top, rows).T
    listing = listing[jax.random.permutation(jax.random.fold_in(own, 1), rows)]
    rotation = jax.random.randint(jax.random.fold_in(own, 2), (rows, 1), 0, top)
    return jnp.take_along_axis(listing, (jnp.arange(top)[None, :] + rotation) % top, axis=1)


def load_shares(amount, total, most, slope, full):
    portions = [(1 << 20) // math.isqrt(rank ** slope) + 1 for rank in range(1, amount + 1)]
    largest = most if full else min(most, max(-(-total // amount), total * portions[0] // sum(portions)))
    least = 1 if total - largest >= amount - 1 else 0
    given, spare = [largest] + [least] * (amount - 1), total - largest - least * (amount - 1)
    while spare > 0:
        candidates = [i for i in range(1, amount) if given[i] < largest] or [i for i in range(1, amount) if given[i] < most]
        whole, budget = sum([portions[i] for i in candidates]), spare
        for i in candidates:
            addition = min(most - given[i], max(1, budget * portions[i] // whole), spare)
            given[i] = given[i] + addition
            spare = spare - addition
    return np.array(given)


def bell_draw(stream_key, extent, scale, bound, cuts=(), held_as=jnp.bfloat16):
    drawn = scale * jax.random.normal(stream_key, extent, jnp.float32)
    if cuts:
        drawn = drawn * shard_levels(stream_key, extent, cuts, -0.22, 0.18)
    return jnp.clip(drawn, -bound, bound).astype(held_as)


def setup_inputs(seed: int = 0) -> dict:
    seeds = jax.random.split(jax.random.key(seed), 13)
    velocity = bell_draw(seeds[0], (3, NX, NY, NZ), 1.0, 6.0, ((1, 8), (2, 16)), jnp.float32)
    stress = bell_draw(seeds[1], (6, NX, NY, NZ), 1.0, 6.0, ((1, 8), (2, 16)), jnp.float32)
    region_id = with_ends(jax.random.randint(seeds[2], (NX, NY, NZ), 0, REGIONS), jax.random.fold_in(seeds[2], 1), 0, REGIONS - 1).astype(jnp.int32)
    buoyancy = jnp.clip(jnp.exp(jax.random.uniform(seeds[3], (REGIONS,), jnp.float32, math.log(0.5), math.log(1.0))), 0.5, 1.0)
    lame_lambda = jnp.clip(jnp.exp(jax.random.uniform(seeds[4], (REGIONS,), jnp.float32, math.log(0.5), math.log(2.0))), 0.5, 2.0)
    shear_mu = jnp.clip(jnp.exp(jax.random.uniform(seeds[5], (REGIONS,), jnp.float32, math.log(0.25), math.log(1.0))), 0.25, 1.0)
    shell_rows = bell_draw(seeds[6], (SHELL, 9, NZ), 1.0, 6.0, ((0, 128),), jnp.float32)
    shell_target_keys = jax.random.split(jax.random.fold_in(seeds[7], 1), SHELL // SH_DEV)
    shell_target_turns = jax.random.permutation(jax.random.fold_in(seeds[7], 3), SHELL // SH_DEV)
    shell_target = jax.vmap(lambda own, number: assign_block(jax.random.fold_in(seeds[7], 2), own, number, SH_DEV, DEVICES, 1, CAP, 2))(shell_target_keys, shell_target_turns).reshape((SHELL, 1))
    shell_cell = with_ends(jax.random.randint(seeds[8], (SHELL, 1), 0, CX * CY), jax.random.fold_in(seeds[8], 1), 0, (CX * CY) - 1).astype(jnp.int32)
    pile_pier_keys = jax.random.split(jax.random.fold_in(seeds[9], 1), PILES // PILE_DEV)
    pile_pier_turns = jax.random.permutation(jax.random.fold_in(seeds[9], 3), PILES // PILE_DEV)
    pile_pier = jax.vmap(lambda own, number: assign_block(jax.random.fold_in(seeds[9], 2), own, number, PILE_DEV, PIERS, 1, CAPP, 2))(pile_pier_keys, pile_pier_turns).reshape((PILES, 1))
    pile_cell = with_ends(jax.random.randint(seeds[10], (PILES, 1), 0, CX * CY), jax.random.fold_in(seeds[10], 1), 0, (CX * CY) - 1).astype(jnp.int32)
    pier_owner = jax.random.permutation(seeds[11], PIERS).astype(jnp.int32)
    return dict(velocity=velocity, stress=stress, region_id=region_id, buoyancy=buoyancy, lame_lambda=lame_lambda, shear_mu=shear_mu, shell_rows=shell_rows, shell_target=shell_target, shell_cell=shell_cell, pile_pier=pile_pier, pile_cell=pile_cell, pier_owner=pier_owner)


STEP = 0.25
DAMP = 0.3


def absorb(distance):
    ramp = jnp.maximum(0.0, (PML - distance) / PML)
    return 1.0 - DAMP * ramp * ramp


def damping(x_index, x_total, y_index, y_total, depth):
    along_x = absorb(jnp.minimum(x_index, x_total - 1 - x_index).astype(jnp.float32))
    along_y = absorb(jnp.minimum(y_index, y_total - 1 - y_index).astype(jnp.float32))
    depth_index = jnp.arange(depth, dtype=jnp.int32)
    along_z = absorb((depth - 1 - depth_index).astype(jnp.float32))
    return along_x[:, None, None] * along_y[None, :, None] * along_z[None, None, :]


def shift_up(values):
    return jnp.concatenate([values[..., 1:], jnp.zeros_like(values[..., :1])], axis=-1) - values


def shift_down(values):
    return values - jnp.concatenate([jnp.zeros_like(values[..., :1]), values[..., :-1]], axis=-1)


def differences(padded):
    middle = padded[:, 1:-1, 1:-1]

    def ahead_x(field):
        return padded[field, 2:, 1:-1] - middle[field]

    def behind_x(field):
        return middle[field] - padded[field, :-2, 1:-1]

    def ahead_y(field):
        return padded[field, 1:-1, 2:] - middle[field]

    def behind_y(field):
        return middle[field] - padded[field, 1:-1, :-2]

    return middle, ahead_x, behind_x, ahead_y, behind_y


def move_velocity(velocity, padded, buoyant):
    middle, ahead_x, behind_x, ahead_y, behind_y = differences(padded)
    scaled = STEP * buoyant
    velocity_x = velocity[0] + scaled * (ahead_x(0) + behind_y(3) + shift_down(middle[4]))
    velocity_y = velocity[1] + scaled * (behind_x(3) + ahead_y(1) + shift_down(middle[5]))
    velocity_z = velocity[2] + scaled * (behind_x(4) + behind_y(5) + shift_up(middle[2]))
    return jnp.stack([velocity_x, velocity_y, velocity_z])


def move_stress(stress, padded, lame_first, shear_cells):
    middle, ahead_x, behind_x, ahead_y, behind_y = differences(padded)
    strain_xx = behind_x(0)
    strain_yy = behind_y(1)
    strain_zz = shift_down(middle[2])
    dilation = strain_xx + strain_yy + strain_zz
    stress_xx = stress[0] + STEP * (lame_first * dilation + 2.0 * shear_cells * strain_xx)
    stress_yy = stress[1] + STEP * (lame_first * dilation + 2.0 * shear_cells * strain_yy)
    stress_zz = stress[2] + STEP * (lame_first * dilation + 2.0 * shear_cells * strain_zz)
    stress_xy = stress[3] + STEP * shear_cells * (ahead_x(1) + ahead_y(0))
    stress_xz = stress[4] + STEP * shear_cells * (ahead_x(2) + shift_up(middle[0]))
    stress_yz = stress[5] + STEP * shear_cells * (ahead_y(2) + shift_up(middle[1]))
    return jnp.stack([stress_xx, stress_yy, stress_zz, stress_xy, stress_xz, stress_yz])


def reference(velocity, stress, region_id, buoyancy, lame_lambda, shear_mu, shell_rows, shell_target, shell_cell, pile_pier, pile_cell, pier_owner):
    columns = NX * NY
    target = shell_target[:, 0]
    local_cell = shell_cell[:, 0]
    shell_x = (target // N_GY) * CX + local_cell // CY
    shell_y = (target % N_GY) * CY + local_cell % CY
    shell_column = (shell_x * NY + shell_y).astype(jnp.int32)
    rows_moved = jnp.transpose(shell_rows, (1, 0, 2))
    velocity_in = velocity.reshape(3, columns, NZ).at[:, shell_column].add(rows_moved[:3]).reshape(3, NX, NY, NZ)
    stress_in = stress.reshape(6, columns, NZ).at[:, shell_column].add(rows_moved[3:]).reshape(6, NX, NY, NZ)
    buoyant = buoyancy[region_id]
    lame_first = lame_lambda[region_id]
    shear_cells = shear_mu[region_id]
    widths = ((0, 0), (1, 1), (1, 1), (0, 0))
    velocity_new = move_velocity(velocity_in, jnp.pad(stress_in, widths), buoyant)
    stress_new = move_stress(stress_in, jnp.pad(velocity_new, widths), lame_first, shear_cells)
    factor = damping(jnp.arange(NX, dtype=jnp.int32), NX, jnp.arange(NY, dtype=jnp.int32), NY, NZ)
    velocity_out = velocity_new * factor
    stress_out = stress_new * factor
    source = jnp.arange(PILES, dtype=jnp.int32) // PILE_DEV
    pile_local = pile_cell[:, 0]
    pile_x = (source // N_GY) * CX + pile_local // CY
    pile_y = (source % N_GY) * CY + pile_local % CY
    pile_column = (pile_x * NY + pile_y).astype(jnp.int32)
    traction = jnp.stack([stress_out[4], stress_out[5], stress_out[2]]).reshape(3, columns, NZ)[:, pile_column]
    response = jnp.tanh(jnp.transpose(traction, (1, 0, 2)))
    owner_slot = pier_owner[pile_pier[:, 0]]
    summed = jnp.zeros((PIERS, 3, NZ), jnp.float32).at[owner_slot].add(response)
    pier_force = (summed * (PIER_DEV / PILE_DEV) ** 0.5).reshape(PIERS, 3 * NZ)
    return velocity_out, stress_out, pier_force
```

```python
import functools

import jax
import jax.numpy as jnp
from jax import lax
from jax.experimental import pallas as pl
from jax.experimental.pallas import tpu as pltpu
from jax.sharding import PartitionSpec as P

PML = 8
STEP = 0.25
DAMP = 0.3
SLOTS = 4
GROUPS = 4
MESH = pl.DeviceIdType.MESH
F32 = jnp.float32
BF16 = jnp.bfloat16


def iota(shape, dim):
    return lax.broadcasted_iota(jnp.int32, shape, dim)


def split_in_two(values):
    high = values.astype(BF16)
    return high, (values - high.astype(F32)).astype(BF16)


def absorb(distance):
    ramp = jnp.maximum(0.0, (PML - distance) / PML)
    return 1.0 - DAMP * ramp * ramp


def z_before(field):
    return jnp.where(iota(field.shape, 1) == 0, 0.0, pltpu.roll(field, 1, 1))


def z_after(field):
    size = field.shape[1]
    return jnp.where(iota(field.shape, 1) == size - 1, 0.0, pltpu.roll(field, size - 1, 1))


def y_before(field):
    return jnp.where(iota(field.shape, 0) == 0, 0.0, pltpu.roll(field, 1, 0))


def y_after(field):
    size = field.shape[0]
    return jnp.where(iota(field.shape, 0) == size - 1, 0.0, pltpu.roll(field, size - 1, 0))


def column_of(row):
    size = row.shape[1]
    square = iota((size, size), 0) == iota((size, size), 1)
    return jnp.sum(jnp.where(square, row.astype(F32), 0.0), axis=1, keepdims=True)


def lookup(region, table_ref):
    values = [table_ref[i] for i in range(16)]
    for bit in range(4):
        mask = (region & (1 << bit)) != 0
        values = [jnp.where(mask, values[2 * i + 1], values[2 * i]) for i in range(len(values) // 2)]
    return values[0]


def peer(step, gx, gy):
    x = (gx + step) % 4
    y = (gy // 2 + step // 4 + step) % 4
    z = (gx // 4 + 2 * (gy // 8) + step // 16 + step) % 4
    core = (gy + step // 64 + step) % 2
    return (z % 2) * 4 + x, (z // 2) * 8 + y * 2 + core


def wave_kernel(
    target, cell, table_b, table_l, table_m, rows_in, velocity_in, stress_in, region_in,
    vel, st,
    rows, region, hb, hl, hm, parts, outgoing, arrived, group, y_send, x_halo, y_halo, v_send, vx_halo, vy_halo,
    load_sem, own_sem, send_sem, recv_sem, halo_send, halo_recv,
):
    gx, gy = lax.axis_index("gx"), lax.axis_index("gy")
    count_x, count_y = 8, 16
    devices = count_x * count_y
    me = gx * count_y + gy
    load_rows = pltpu.make_async_copy(rows_in, rows, load_sem.at[0])
    load_rows.start()
    load_region = pltpu.make_async_copy(region_in, region, load_sem.at[1])
    load_vel = pltpu.make_async_copy(velocity_in, vel, load_sem.at[2])
    load_st = pltpu.make_async_copy(stress_in, st, load_sem.at[3])
    load_region.start()
    load_vel.start()
    load_st.start()

    barrier = pltpu.get_barrier_semaphore()

    def greet(step, _):
        other = lax.rem(me + step, devices)
        pl.semaphore_signal(
            barrier, inc=1, device_id=(other // count_y, other % count_y), device_id_type=MESH
        )
        return 0

    lax.fori_loop(1, devices, greet, 0)

    target_row = target[...]
    count = target_row.shape[1]
    target_col = column_of(target_row).astype(jnp.int32)
    same = (target_col == target_row) & (iota((count, count), 0) < iota((count, count), 1))
    rank_row = jnp.sum(jnp.where(same, 1.0, 0.0), axis=0, keepdims=True)
    cell_row = cell[...].astype(F32)
    load_rows.wait()
    for f in range(9):
        high, low = split_in_two(rows[f])
        parts[0:count, f * 128 : (f + 1) * 128] = high
        parts[count : 2 * count, f * 128 : (f + 1) * 128] = low
    named = target_row == iota((devices, count), 0)
    cells_out = jnp.zeros((devices, 128), F32)
    lane_slot = iota((devices, 128), 1) // 32
    for k in range(SLOTS):
        mine = named & (rank_row == float(k))
        pick = jnp.where(mine, 1.0, 0.0).astype(BF16)
        pick = jnp.concatenate([pick, pick], axis=1)
        cell_col = jnp.sum(jnp.where(mine, cell_row, 0.0), axis=1, keepdims=True)
        cells_out = jnp.where(lane_slot == k, cell_col, cells_out)
        for first in range(0, 9, 2):
            width = min(2, 9 - first)
            packed = jnp.dot(
                pick, parts[:, first * 128 : (first + width) * 128], preferred_element_type=F32
            )
            for f in range(width):
                outgoing[(first + f) * SLOTS + k] = packed[:, f * 128 : (f + 1) * 128]
    outgoing[9 * SLOTS] = cells_out

    pl.semaphore_wait(barrier, devices - 1)
    per_group = devices // GROUPS

    def send(step, _):
        to_x, to_y = peer(step, gx, gy)
        pltpu.make_async_remote_copy(
            src_ref=outgoing.at[:, to_x * count_y + to_y, :],
            dst_ref=arrived.at[:, step, :],
            send_sem=send_sem,
            recv_sem=recv_sem.at[step // per_group],
            device_id=(to_x, to_y),
            device_id_type=MESH,
        ).start()
        return 0

    lax.fori_loop(1, devices, send, 0)
    own = pltpu.make_async_copy(outgoing.at[:, me, :], arrived.at[:, 0, :], own_sem)
    own.start()

    load_region.wait()

    def materials(x, _):
        here = region[x]
        hb[x] = STEP * lookup(here, table_b)
        hl[x] = STEP * lookup(here, table_l)
        hm[x] = STEP * lookup(here, table_m)
        return 0

    lax.fori_loop(0, 32, materials, 0)
    load_vel.wait()
    load_st.wait()
    own.wait()

    def add_group(g, first):
        for f in range(9):
            for k in range(SLOTS):
                high, low = split_in_two(arrived[f * SLOTS + k, pl.ds(first, 32), :])
                group[k * 32 : (k + 1) * 32, f * 128 : (f + 1) * 128] = high
                group[128 + k * 32 : 128 + (k + 1) * 32, f * 128 : (f + 1) * 128] = low
        names = arrived[9 * SLOTS, pl.ds(first, 32), :]
        mine = iota((32, 128), 1) % 32 == iota((32, 128), 0)
        names = jnp.sum(jnp.where(mine, names, 0.0), axis=0, keepdims=True).astype(jnp.int32)
        names = jnp.concatenate([names, names], axis=1)

        def add_block(block, _):
            pick = jnp.where(iota((256, 256), 0) + block * 256 == names, 1.0, 0.0).astype(BF16)
            for first in range(0, 9, 2):
                width = min(2, 9 - first)
                added = jnp.dot(
                    pick, group[:, first * 128 : (first + width) * 128], preferred_element_type=F32
                )
                for f in range(width):
                    piece = added[:, f * 128 : (f + 1) * 128].reshape(4, 64, 128)
                    if first + f < 3:
                        vel[first + f, pl.ds(block * 4, 4)] += piece
                    else:
                        st[first + f - 3, pl.ds(block * 4, 4)] += piece
            return 0

        lax.fori_loop(0, 8, add_block, 0)

    for g in range(GROUPS):
        low = 1 if g == 0 else 0
        landed = arrived.at[:, pl.ds(g * per_group + low, per_group - low), :]
        pltpu.make_async_remote_copy(
            src_ref=landed, dst_ref=landed, send_sem=send_sem, recv_sem=recv_sem.at[g],
            device_id=(gx, gy), device_id_type=MESH,
        ).wait_recv()
        add_group(g, g * per_group)

    x_after_dev = ((gx + 1) % count_x, gy)
    x_before_dev = ((gx + count_x - 1) % count_x, gy)
    y_after_dev = (gx, (gy + 1) % count_y)
    y_before_dev = (gx, (gy + count_y - 1) % count_y)
    has_x_before, has_x_after = gx > 0, gx < count_x - 1
    has_y_before, has_y_after = gy > 0, gy < count_y - 1

    def halo_copy(number, source, landing, device):
        return pltpu.make_async_remote_copy(
            src_ref=source, dst_ref=landing, send_sem=halo_send.at[number],
            recv_sem=halo_recv.at[number], device_id=device, device_id_type=MESH,
        )

    y_send[0] = st[3, :, 63:64, :]
    y_send[1] = st[5, :, 63:64, :]
    y_send[2] = st[1, :, 0:1, :]
    stress_copies = [
        halo_copy(0, st.at[0, 0], x_halo.at[0], x_before_dev),
        halo_copy(1, st.at[pl.ds(3, 2), 31], x_halo.at[pl.ds(1, 2)], x_after_dev),
        halo_copy(2, y_send.at[pl.ds(0, 2)], y_halo.at[pl.ds(0, 2)], y_after_dev),
        halo_copy(3, y_send.at[2], y_halo.at[2], y_before_dev),
    ]
    for copy in stress_copies:
        copy.start()

    def move_velocity(x, xx_after, xy_before, xz_before):
        xx, yy, zz, xy, xz, yz = [st[f, x] for f in range(6)]
        scaled = hb[x]
        vel[0, x] += scaled * ((xx_after - xx) + (xy - y_before(xy)) + (xz - z_before(xz)))
        vel[1, x] += scaled * ((xy - xy_before) + (y_after(yy) - yy) + (yz - z_before(yz)))
        vel[2, x] += scaled * ((xz - xz_before) + (yz - y_before(yz)) + (z_after(zz) - zz))

    def inner_velocity(x, _):
        move_velocity(x, st[0, x + 1], st[3, x - 1], st[4, x - 1])
        return 0

    lax.fori_loop(1, 31, inner_velocity, 0)
    for copy in stress_copies:
        copy.wait()
    move_velocity(
        0, st[0, 1], jnp.where(has_x_before, x_halo[1], 0.0), jnp.where(has_x_before, x_halo[2], 0.0)
    )
    move_velocity(31, jnp.where(has_x_after, x_halo[0], 0.0), st[3, 30], st[4, 30])
    top, bottom = hb[:, 0:1, :], hb[:, 63:64, :]
    vel[0, :, 0:1, :] -= top * jnp.where(has_y_before, y_halo[0], 0.0)
    vel[2, :, 0:1, :] -= top * jnp.where(has_y_before, y_halo[1], 0.0)
    vel[1, :, 63:64, :] += bottom * jnp.where(has_y_after, y_halo[2], 0.0)

    v_send[0] = vel[1, :, 63:64, :]
    v_send[1] = vel[0, :, 0:1, :]
    v_send[2] = vel[2, :, 0:1, :]
    velocity_copies = [
        halo_copy(4, vel.at[0, 31], vx_halo.at[0], x_after_dev),
        halo_copy(5, vel.at[pl.ds(1, 2), 0], vx_halo.at[pl.ds(1, 2)], x_before_dev),
        halo_copy(6, v_send.at[0], vy_halo.at[0], y_after_dev),
        halo_copy(7, v_send.at[pl.ds(1, 2)], vy_halo.at[pl.ds(1, 2)], y_before_dev),
    ]
    for copy in velocity_copies:
        copy.start()

    def move_stress(x, vx_before, vy_after, vz_after):
        vx, vy, vz = [vel[c, x] for c in range(3)]
        first, shear = hl[x], hm[x]
        strain_x, strain_y, strain_z = vx - vx_before, vy - y_before(vy), vz - z_before(vz)
        spread = first * (strain_x + strain_y + strain_z)
        twice = 2.0 * shear
        st[0, x] += spread + twice * strain_x
        st[1, x] += spread + twice * strain_y
        st[2, x] += spread + twice * strain_z
        st[3, x] += shear * ((vy_after - vy) + (y_after(vx) - vx))
        st[4, x] += shear * ((vz_after - vz) + (z_after(vx) - vx))
        st[5, x] += shear * ((y_after(vz) - vz) + (z_after(vy) - vy))

    def inner_stress(x, _):
        move_stress(x, vel[0, x - 1], vel[1, x + 1], vel[2, x + 1])
        return 0

    lax.fori_loop(1, 31, inner_stress, 0)
    for copy in velocity_copies:
        copy.wait()
    move_stress(0, jnp.where(has_x_before, vx_halo[0], 0.0), vel[1, 1], vel[2, 1])
    move_stress(
        31, vel[0, 30], jnp.where(has_x_after, vx_halo[1], 0.0), jnp.where(has_x_after, vx_halo[2], 0.0)
    )
    vy_edge = jnp.where(has_y_before, vy_halo[0], 0.0)
    first, shear = hl[:, 0:1, :], hm[:, 0:1, :]
    st[0, :, 0:1, :] -= first * vy_edge
    st[1, :, 0:1, :] -= (first + 2.0 * shear) * vy_edge
    st[2, :, 0:1, :] -= first * vy_edge
    shear = hm[:, 63:64, :]
    st[3, :, 63:64, :] += shear * jnp.where(has_y_after, vy_halo[1], 0.0)
    st[5, :, 63:64, :] += shear * jnp.where(has_y_after, vy_halo[2], 0.0)

    sent = outgoing.at[:, pl.ds(0, devices - 1), :]
    pltpu.make_async_remote_copy(
        src_ref=sent, dst_ref=sent, send_sem=send_sem, recv_sem=recv_sem.at[0],
        device_id=(gx, gy), device_id_type=MESH,
    ).wait_send()


def finish_kernel(
    pile_cell, vel, st, pile_pier, owner, vel_out, st_out, partial, damped_v, damped_s, traction, sems
):
    gx, gy = lax.axis_index("gx"), lax.axis_index("gy")
    y_index = gy * 64 + iota((64, 128), 0)
    along_y = absorb(jnp.minimum(y_index, 1023 - y_index).astype(F32))
    along_z = absorb((127 - iota((64, 128), 1)).astype(F32))
    plane = along_y * along_z

    def damp(step, _):
        for i in range(4):
            x = step * 4 + i
            x_index = gx * 32 + x
            far = jnp.broadcast_to(jnp.minimum(x_index, 255 - x_index), (64, 128)).astype(F32)
            factor = absorb(far) * plane
            for c in range(3):
                damped_v[c, x] = vel[c, x] * factor
            for f in range(6):
                damped_s[f, x] = st[f, x] * factor
        planes = pl.ds(step * 4, 4)
        pltpu.make_async_copy(damped_v.at[:, planes], vel_out.at[:, planes], sems.at[0]).start()
        pltpu.make_async_copy(damped_s.at[:, planes], st_out.at[:, planes], sems.at[1]).start()
        return 0

    lax.fori_loop(0, 8, damp, 0)

    def fetch(p, _):
        at = pile_cell[p]
        x, y = at // 64, at % 64
        for c, f in enumerate((4, 5, 2)):
            traction[c, pl.ds(p, 1), :] = damped_s[f, x, pl.ds(y, 1), :]
        return 0

    lax.fori_loop(0, 256, fetch, 0, unroll=8)
    pier_row = pile_pier[...]
    owner_col = column_of(owner[...])
    named = pier_row == iota((128, 256), 0)
    slot_row = jnp.sum(jnp.where(named, owner_col, 0.0), axis=0, keepdims=True).astype(jnp.int32)
    pick = jnp.where(slot_row == iota((128, 256), 0), 1.0, 0.0).astype(BF16)
    pick = jnp.concatenate([pick, pick], axis=1)
    response = jnp.concatenate([jnp.tanh(traction[c]) for c in range(3)], axis=1)
    high, low = split_in_two(response)
    both = jnp.concatenate([high, low], axis=0)
    partial[...] = jnp.dot(pick, both, preferred_element_type=F32)
    pltpu.make_async_copy(damped_v, vel_out, sems.at[0]).wait()
    pltpu.make_async_copy(damped_s, st_out, sems.at[1]).wait()


def pier_kernel(partial, force, first, second, rows, send_one, recv_one, send_two, recv_two):
    gx, gy = lax.axis_index("gx"), lax.axis_index("gy")
    barrier = pltpu.get_barrier_semaphore()
    for k in range(1, 8):
        pl.semaphore_signal(barrier, inc=1, device_id=((gx + k) % 8, gy), device_id_type=MESH)
    for k in range(1, 16):
        pl.semaphore_signal(barrier, inc=1, device_id=(gx, (gy + k) % 16), device_id_type=MESH)
    pl.semaphore_wait(barrier, 22)

    copies = []
    for k in range(1, 8):
        to = (gx + k) % 8
        copies.append(
            pltpu.make_async_remote_copy(
                src_ref=partial.at[pl.ds(pl.multiple_of(to * 16, 16), 16)],
                dst_ref=first.at[k - 1],
                send_sem=send_one.at[k - 1],
                recv_sem=recv_one.at[k - 1],
                device_id=(to, gy),
                device_id_type=MESH,
            )
        )
    for copy in copies:
        copy.start()
    total = partial[pl.ds(pl.multiple_of(gx * 16, 16), 16), :]
    for k, copy in enumerate(copies):
        copy.wait_recv()
        total = total + first[k]
    for j in range(16):
        rows[j] = total[j : j + 1, :]
    more = []
    for k in range(1, 16):
        to = (gy + k) % 16
        more.append(
            pltpu.make_async_remote_copy(
                src_ref=rows.at[to],
                dst_ref=second.at[k - 1],
                send_sem=send_two.at[k - 1],
                recv_sem=recv_two.at[k - 1],
                device_id=(gx, to),
                device_id_type=MESH,
            )
        )
    for copy in more:
        copy.start()
    result = rows[gy]
    for k, copy in enumerate(more):
        copy.wait_recv()
        result = result + second[k]
    force[...] = result * (1.0 / 256.0) ** 0.5
    for copy in copies + more:
        copy.wait_send()


def on_device(
    velocity,
    stress,
    region_id,
    buoyancy,
    lame_lambda,
    shear_mu,
    shell_rows,
    shell_target,
    shell_cell,
    pile_pier,
    pile_cell,
    pier_owner,
):
    vmem = pl.BlockSpec(memory_space=pltpu.VMEM)
    smem = pl.BlockSpec(memory_space=pltpu.SMEM)
    anywhere = pl.BlockSpec(memory_space=pl.ANY)
    dma = pltpu.SemaphoreType.DMA
    vel, st = pl.pallas_call(
        wave_kernel,
        out_shape=(pltpu.VMEM((3, 32, 64, 128), F32), pltpu.VMEM((6, 32, 64, 128), F32)),
        in_specs=[vmem, vmem, smem, smem, smem, anywhere, anywhere, anywhere, anywhere],
        out_specs=(vmem, vmem),
        scratch_shapes=[
            pltpu.VMEM((9, 256, 128), F32),
            pltpu.VMEM((32, 64, 128), jnp.int32),
            pltpu.VMEM((32, 64, 128), F32),
            pltpu.VMEM((32, 64, 128), F32),
            pltpu.VMEM((32, 64, 128), F32),
            pltpu.VMEM((512, 1152), BF16),
            pltpu.VMEM((37, 128, 128), F32),
            pltpu.VMEM((37, 128, 128), F32),
            pltpu.VMEM((256, 1152), BF16),
            pltpu.VMEM((3, 32, 1, 128), F32),
            pltpu.VMEM((3, 64, 128), F32),
            pltpu.VMEM((3, 32, 1, 128), F32),
            pltpu.VMEM((3, 32, 1, 128), F32),
            pltpu.VMEM((3, 64, 128), F32),
            pltpu.VMEM((3, 32, 1, 128), F32),
            dma((4,)),
            dma,
            dma,
            dma((GROUPS,)),
            dma((8,)),
            dma((8,)),
        ],
        compiler_params=pltpu.CompilerParams(
            collective_id=0, has_side_effects=True, vmem_limit_bytes=40 << 20
        ),
    )(
        shell_target.reshape(1, 256),
        shell_cell.reshape(1, 256),
        buoyancy,
        lame_lambda,
        shear_mu,
        jnp.transpose(shell_rows, (1, 0, 2)),
        velocity,
        stress,
        region_id,
    )
    velocity_out, stress_out, partial = pl.pallas_call(
        finish_kernel,
        out_shape=(
            jax.ShapeDtypeStruct((3, 32, 64, 128), F32),
            jax.ShapeDtypeStruct((6, 32, 64, 128), F32),
            jax.ShapeDtypeStruct((128, 384), F32),
        ),
        in_specs=[smem, vmem, vmem, vmem, vmem],
        out_specs=(anywhere, anywhere, vmem),
        scratch_shapes=[
            pltpu.VMEM((3, 32, 64, 128), F32),
            pltpu.VMEM((6, 32, 64, 128), F32),
            pltpu.VMEM((3, 256, 128), F32),
            dma((2,)),
        ],
        compiler_params=pltpu.CompilerParams(vmem_limit_bytes=40 << 20),
    )(
        pile_cell.reshape(256),
        vel,
        st,
        pile_pier.reshape(1, 256),
        pier_owner.reshape(1, 128),
    )
    pier_force = pl.pallas_call(
        pier_kernel,
        out_shape=jax.ShapeDtypeStruct((1, 384), F32),
        in_specs=[vmem],
        out_specs=vmem,
        scratch_shapes=[
            pltpu.VMEM((7, 16, 384), F32),
            pltpu.VMEM((15, 1, 384), F32),
            pltpu.VMEM((16, 1, 384), F32),
            dma((7,)),
            dma((7,)),
            dma((15,)),
            dma((15,)),
        ],
        compiler_params=pltpu.CompilerParams(collective_id=1, has_side_effects=True),
    )(partial)
    return velocity_out, stress_out, pier_force


def solution(mesh):
    return jax.shard_map(
        on_device,
        mesh=mesh,
        in_specs=(
            P(None, "gx", "gy", None),
            P(None, "gx", "gy", None),
            P("gx", "gy", None),
            P(),
            P(),
            P(),
            P(("gx", "gy"), None, None),
            P(("gx", "gy"), None),
            P(("gx", "gy"), None),
            P(("gx", "gy"), None),
            P(("gx", "gy"), None),
            P(),
        ),
        out_specs=(P(None, "gx", "gy", None), P(None, "gx", "gy", None), P(("gx", "gy"), None)),
        check_vma=False,
    )
```

```python
import functools

import jax
import jax.numpy as jnp
from jax import lax
from jax.experimental import pallas as pl
from jax.experimental.pallas import tpu as pltpu
from jax.sharding import PartitionSpec as P

PML = 8
STEP = 0.25
DAMP = 0.3
SLOTS = 4
GROUPS = 4
UNROLL = 4
MESH = pl.DeviceIdType.MESH
LOGICAL = pl.DeviceIdType.LOGICAL
F32 = jnp.float32
BF16 = jnp.bfloat16


def iota(shape, dim):
    return lax.broadcasted_iota(jnp.int32, shape, dim)


def split_in_two(values):
    high = values.astype(BF16)
    return high, (values - high.astype(F32)).astype(BF16)


def absorb(distance):
    ramp = jnp.maximum(0.0, (PML - distance) / PML)
    return 1.0 - DAMP * ramp * ramp


def z_before(field):
    return jnp.where(iota(field.shape, 1) == 0, 0.0, pltpu.roll(field, 1, 1))


def z_after(field):
    size = field.shape[1]
    return jnp.where(iota(field.shape, 1) == size - 1, 0.0, pltpu.roll(field, size - 1, 1))


def y_before(field):
    return jnp.where(iota(field.shape, 0) == 0, 0.0, pltpu.roll(field, 1, 0))


def y_after(field):
    size = field.shape[0]
    return jnp.where(iota(field.shape, 0) == size - 1, 0.0, pltpu.roll(field, size - 1, 0))


def column_of(row):
    size = row.shape[1]
    square = iota((size, size), 0) == iota((size, size), 1)
    return jnp.sum(jnp.where(square, row.astype(F32), 0.0), axis=1, keepdims=True)


def lookup(region, table_ref):
    values = [table_ref[i] for i in range(16)]
    for bit in range(4):
        mask = (region & (1 << bit)) != 0
        values = [jnp.where(mask, values[2 * i + 1], values[2 * i]) for i in range(len(values) // 2)]
    return values[0]


def peer(step, gx, gy):
    x = lax.rem(gx + step, 4)
    y = lax.rem(lax.div(gy, 2) + lax.div(step, 4) + step, 4)
    z = lax.rem(lax.div(gx, 4) + 2 * lax.div(gy, 8) + lax.div(step, 16) + step, 4)
    core = lax.rem(gy + lax.div(step, 64) + step, 2)
    return lax.rem(z, 2) * 64 + x * 16 + lax.div(z, 2) * 8 + y * 2 + core


def wave_kernel(
    target_in, cell_in, table_b_in, table_l_in, table_m_in, rows_in, velocity_in, stress_in, region_in,
    pile_cell_in, pile_pier_in, owner_in,
    vel, st, force,
    target, cell, table_b, table_l, table_m, rows, region, hb, hl, hm,
    pile_at, pile_cell, pile_pier, owner, traction, response, sums, sums_in,
    parts, outgoing, arrived, group, x_send, y_send, x_halo, y_halo, v_send, vx_halo, vy_halo,
    load_sem, own_sem, send_sem, recv_sem, halo_send, halo_recv, sums_send, sums_recv,
):
    gx, gy = lax.axis_index("gx"), lax.axis_index("gy")
    count_x, count_y = 8, 16
    devices = count_x * count_y
    me = gx * count_y + gy
    loads = [
        pltpu.make_async_copy(source, landing, load_sem.at[i])
        for i, (source, landing) in enumerate((
            (target_in, target), (cell_in, cell), (rows_in, rows),
            (table_b_in, table_b), (table_l_in, table_l), (table_m_in, table_m), (region_in, region),
            (velocity_in, vel), (stress_in, st), (pile_cell_in, pile_at), (pile_cell_in, pile_cell),
            (pile_pier_in, pile_pier), (owner_in, owner),
        ))
    ]
    for load in loads:
        load.start()

    barrier = pltpu.get_barrier_semaphore()

    def greet(step, _):
        pl.semaphore_signal(
            barrier, inc=1, device_id=lax.rem(me + step, devices), device_id_type=LOGICAL
        )
        return 0

    lax.fori_loop(1, devices, greet, 0, unroll=8)
    for load in loads[:3]:
        load.wait()

    target_row = target[...]
    count = target_row.shape[1]
    target_col = column_of(target_row).astype(jnp.int32)
    same = (target_col == target_row) & (iota((count, count), 0) < iota((count, count), 1))
    rank_row = jnp.sum(jnp.where(same, 1.0, 0.0), axis=0, keepdims=True)
    cell_row = cell[...].astype(F32)
    for f in range(9):
        high, low = split_in_two(rows[f])
        parts[0:count, f * 128 : (f + 1) * 128] = high
        parts[count : 2 * count, f * 128 : (f + 1) * 128] = low
    named = target_row == iota((devices, count), 0)
    cells_out = jnp.zeros((devices, 128), F32)
    lane_slot = iota((devices, 128), 1) // 32
    for k in range(SLOTS):
        mine = named & (rank_row == float(k))
        pick = jnp.where(mine, 1.0, 0.0).astype(BF16)
        pick = jnp.concatenate([pick, pick], axis=1)
        cell_col = jnp.sum(jnp.where(mine, cell_row, 0.0), axis=1, keepdims=True)
        cells_out = jnp.where(lane_slot == k, cell_col, cells_out)
        for first in range(0, 9, 2):
            width = min(2, 9 - first)
            packed = jnp.dot(
                pick, parts[:, first * 128 : (first + width) * 128], preferred_element_type=F32
            )
            for f in range(width):
                outgoing[(first + f) * SLOTS + k] = packed[:, f * 128 : (f + 1) * 128]
    outgoing[9 * SLOTS] = cells_out

    pl.semaphore_wait(barrier, devices - 1)
    per_group = devices // GROUPS

    def send(step, _):
        to = peer(step, gx, gy)
        pltpu.make_async_remote_copy(
            src_ref=outgoing.at[:, to, :],
            dst_ref=arrived.at[:, step, :],
            send_sem=send_sem,
            recv_sem=recv_sem.at[lax.div(step, per_group)],
            device_id=to,
            device_id_type=LOGICAL,
        ).start()
        return 0

    lax.fori_loop(1, devices, send, 0, unroll=8)
    own = pltpu.make_async_copy(outgoing.at[:, me, :], arrived.at[:, 0, :], own_sem)
    own.start()

    for load in loads[3:]:
        load.wait()

    def materials(x, _):
        here = region[x]
        hb[x] = STEP * lookup(here, table_b)
        hl[x] = STEP * lookup(here, table_l)
        hm[x] = STEP * lookup(here, table_m)
        return 0

    lax.fori_loop(0, 32, materials, 0)
    at = column_of(pile_cell[...].reshape(1, 256)).astype(jnp.int32)
    pile_x, pile_y = gx * 32 + at // 64, gy * 64 + at % 64
    plane = absorb(jnp.minimum(pile_x, 255 - pile_x).astype(F32))
    plane = plane * absorb(jnp.minimum(pile_y, 1023 - pile_y).astype(F32))
    pile_factor = plane * absorb((127 - iota((256, 128), 1)).astype(F32))
    owner_col = column_of(owner[...])
    named = pile_pier[...] == iota((devices, 256), 0)
    slot_row = jnp.sum(jnp.where(named, owner_col, 0.0), axis=0, keepdims=True).astype(jnp.int32)
    owned = jnp.where(slot_row == iota((devices, 256), 0), 1.0, 0.0).astype(BF16)
    owned = jnp.concatenate([owned, owned], axis=1)
    own.wait()

    def gather_group(first):
        for f in range(9):
            for k in range(SLOTS):
                high, low = split_in_two(arrived[f * SLOTS + k, pl.ds(first, 32), :])
                group[k * 32 : (k + 1) * 32, f * 128 : (f + 1) * 128] = high
                group[128 + k * 32 : 128 + (k + 1) * 32, f * 128 : (f + 1) * 128] = low
        names = arrived[9 * SLOTS, pl.ds(first, 32), :]
        mine = iota((32, 128), 1) % 32 == iota((32, 128), 0)
        names = jnp.sum(jnp.where(mine, names, 0.0), axis=0, keepdims=True).astype(jnp.int32)
        return jnp.concatenate([names, names], axis=1)

    def add_group(names):
        def add_block(block, _):
            pick = jnp.where(iota((256, 256), 0) + block * 256 == names, 1.0, 0.0).astype(BF16)
            for first in range(0, 9, 2):
                width = min(2, 9 - first)
                added = jnp.dot(
                    pick, group[:, first * 128 : (first + width) * 128], preferred_element_type=F32
                )
                for f in range(width):
                    piece = added[:, f * 128 : (f + 1) * 128].reshape(4, 64, 128)
                    if first + f < 3:
                        vel[first + f, pl.ds(block * 4, 4)] += piece
                    else:
                        st[first + f - 3, pl.ds(block * 4, 4)] += piece
            return 0

        lax.fori_loop(0, 8, add_block, 0, unroll=UNROLL)

    for g in range(GROUPS):
        low = 1 if g == 0 else 0
        landed = arrived.at[:, pl.ds(g * per_group + low, per_group - low), :]
        pltpu.make_async_remote_copy(
            src_ref=landed, dst_ref=landed, send_sem=send_sem, recv_sem=recv_sem.at[g],
            device_id=(gx, gy), device_id_type=MESH,
        ).wait_recv()
        names = gather_group(g * per_group)
        if g < GROUPS - 1:
            add_group(names)

    x_after_dev = ((gx + 1) % count_x, gy)
    x_before_dev = ((gx + count_x - 1) % count_x, gy)
    y_after_dev = (gx, (gy + 1) % count_y)
    y_before_dev = (gx, (gy + count_y - 1) % count_y)
    has_x_before, has_x_after = gx > 0, gx < count_x - 1
    has_y_before, has_y_after = gy > 0, gy < count_y - 1

    def halo_copy(number, source, landing, device):
        return pltpu.make_async_remote_copy(
            src_ref=source, dst_ref=landing, send_sem=halo_send.at[number],
            recv_sem=halo_recv.at[number], device_id=device, device_id_type=MESH,
        )

    row = iota((192, 1), 0)
    column = jnp.where(row < 64, row, row + 31 * 64 - 64)
    column = jnp.where(row >= 128, (row - 128) * 64 + 63, column)
    column = jnp.where(row >= 160, (row - 160) * 64, column)
    pick = jnp.where(column == names, 1.0, 0.0).astype(BF16)
    edge = jnp.dot(pick, group[:, 384:1152], preferred_element_type=F32)
    x_send[0] = st[0, 0] + edge[0:64, 0:128]
    x_send[1] = st[3, 31] + edge[64:128, 384:512]
    x_send[2] = st[4, 31] + edge[64:128, 512:640]
    y_send[0] = st[3, :, 63:64, :] + edge[128:160, 384:512].reshape(32, 1, 128)
    y_send[1] = st[5, :, 63:64, :] + edge[128:160, 640:768].reshape(32, 1, 128)
    y_send[2] = st[1, :, 0:1, :] + edge[160:192, 128:256].reshape(32, 1, 128)
    stress_copies = [
        halo_copy(0, x_send.at[0], x_halo.at[0], x_before_dev),
        halo_copy(1, x_send.at[pl.ds(1, 2)], x_halo.at[pl.ds(1, 2)], x_after_dev),
        halo_copy(2, y_send.at[pl.ds(0, 2)], y_halo.at[pl.ds(0, 2)], y_after_dev),
        halo_copy(3, y_send.at[2], y_halo.at[2], y_before_dev),
    ]
    for copy in stress_copies:
        copy.start()
    add_group(names)

    def move_velocity(x, xx_after, xy_before, xz_before):
        xx, yy, zz, xy, xz, yz = [st[f, x] for f in range(6)]
        scaled = hb[x]
        vel[0, x] += scaled * ((xx_after - xx) + (xy - y_before(xy)) + (xz - z_before(xz)))
        vel[1, x] += scaled * ((xy - xy_before) + (y_after(yy) - yy) + (yz - z_before(yz)))
        vel[2, x] += scaled * ((xz - xz_before) + (yz - y_before(yz)) + (z_after(zz) - zz))

    def inner_velocity(x, _):
        move_velocity(x, st[0, x + 1], st[3, x - 1], st[4, x - 1])
        return 0

    lax.fori_loop(1, 31, inner_velocity, 0, unroll=2)
    for copy in stress_copies:
        copy.wait()
    move_velocity(
        0, st[0, 1], jnp.where(has_x_before, x_halo[1], 0.0), jnp.where(has_x_before, x_halo[2], 0.0)
    )
    move_velocity(31, jnp.where(has_x_after, x_halo[0], 0.0), st[3, 30], st[4, 30])
    top, bottom = hb[:, 0:1, :], hb[:, 63:64, :]
    vel[0, :, 0:1, :] -= top * jnp.where(has_y_before, y_halo[0], 0.0)
    vel[2, :, 0:1, :] -= top * jnp.where(has_y_before, y_halo[1], 0.0)
    vel[1, :, 63:64, :] += bottom * jnp.where(has_y_after, y_halo[2], 0.0)

    v_send[0] = vel[1, :, 63:64, :]
    v_send[1] = vel[0, :, 0:1, :]
    v_send[2] = vel[2, :, 0:1, :]
    velocity_copies = [
        halo_copy(4, vel.at[0, 31], vx_halo.at[0], x_after_dev),
        halo_copy(5, vel.at[pl.ds(1, 2), 0], vx_halo.at[pl.ds(1, 2)], x_before_dev),
        halo_copy(6, v_send.at[0], vy_halo.at[0], y_after_dev),
        halo_copy(7, v_send.at[pl.ds(1, 2)], vy_halo.at[pl.ds(1, 2)], y_before_dev),
    ]
    for copy in velocity_copies:
        copy.start()

    def move_pulled(x, vx_before, vz_after):
        vx, vy, vz = [vel[c, x] for c in range(3)]
        first, shear = hl[x], hm[x]
        strain_z = vz - z_before(vz)
        spread = first * ((vx - vx_before) + (vy - y_before(vy)) + strain_z)
        st[2, x] += spread + 2.0 * shear * strain_z
        st[4, x] += shear * ((vz_after - vz) + (z_after(vx) - vx))
        st[5, x] += shear * ((y_after(vz) - vz) + (z_after(vy) - vy))

    def inner_pulled(x, _):
        move_pulled(x, vel[0, x - 1], vel[2, x + 1])
        return 0

    lax.fori_loop(1, 31, inner_pulled, 0, unroll=2)
    for copy in velocity_copies:
        copy.wait()
    vx_edge = jnp.where(has_x_before, vx_halo[0], 0.0)
    move_pulled(0, vx_edge, vel[2, 1])
    move_pulled(31, vel[0, 30], jnp.where(has_x_after, vx_halo[2], 0.0))
    st[2, :, 0:1, :] -= hl[:, 0:1, :] * jnp.where(has_y_before, vy_halo[0], 0.0)
    st[5, :, 63:64, :] += hm[:, 63:64, :] * jnp.where(has_y_after, vy_halo[2], 0.0)

    def fetch(p, _):
        at = pile_at[p]
        x, y = lax.div(at, 64), lax.rem(at, 64)
        for c, f in enumerate((4, 5, 2)):
            traction[c, pl.ds(p, 1), :] = st[f, x, pl.ds(y, 1), :]
        return 0

    lax.fori_loop(0, 256, fetch, 0, unroll=8)
    for c in range(3):
        high, low = split_in_two(jnp.tanh(traction[c] * pile_factor))
        response[0:256, c * 128 : (c + 1) * 128] = high
        response[256:512, c * 128 : (c + 1) * 128] = low
    total = jnp.dot(owned, response[...], preferred_element_type=F32)
    for c in range(3):
        sums[c] = total[:, c * 128 : (c + 1) * 128]

    def send_sum(step, _):
        to = lax.rem(me + step, devices)
        pltpu.make_async_remote_copy(
            src_ref=sums.at[:, to, :], dst_ref=sums_in.at[:, step, :],
            send_sem=sums_send, recv_sem=sums_recv, device_id=to, device_id_type=LOGICAL,
        ).start()
        return 0

    lax.fori_loop(1, devices, send_sum, 0, unroll=8)
    def move_rest(x, vx_before, vy_after):
        vx, vy, vz = [vel[c, x] for c in range(3)]
        first, shear = hl[x], hm[x]
        row = iota(vx.shape, 0)
        vy_before = jnp.where(row == 0, jnp.where(has_y_before, vy_halo[0, x], 0.0), pltpu.roll(vy, 1, 0))
        vx_after = jnp.where(row == 63, jnp.where(has_y_after, vy_halo[1, x], 0.0), pltpu.roll(vx, 63, 0))
        strain_x, strain_y, strain_z = vx - vx_before, vy - vy_before, vz - z_before(vz)
        spread = first * (strain_x + strain_y + strain_z)
        st[0, x] += spread + 2.0 * shear * strain_x
        st[1, x] += spread + 2.0 * shear * strain_y
        st[3, x] += shear * ((vy_after - vy) + (vx_after - vx))

    def inner_rest(x, _):
        move_rest(x, vel[0, x - 1], vel[1, x + 1])
        return 0

    move_rest(0, vx_edge, vel[1, 1])
    lax.fori_loop(1, 31, inner_rest, 0, unroll=2)
    move_rest(31, vel[0, 30], jnp.where(has_x_after, vx_halo[1], 0.0))

    y_index = gy * 64 + iota((64, 128), 0)
    along_y = absorb(jnp.minimum(y_index, 1023 - y_index).astype(F32))
    factor_yz = along_y * absorb((127 - iota((64, 128), 1)).astype(F32))

    def damp(x, _):
        x_index = gx * 32 + x
        far = jnp.broadcast_to(jnp.minimum(x_index, 255 - x_index), (64, 128)).astype(F32)
        factor = absorb(far) * factor_yz
        for c in range(3):
            vel[c, x] *= factor
        for f in range(6):
            st[f, x] *= factor
        return 0

    lax.fori_loop(0, 32, damp, 0)
    sent = outgoing.at[:, pl.ds(0, devices - 1), :]
    pltpu.make_async_remote_copy(
        src_ref=sent, dst_ref=sent, send_sem=send_sem, recv_sem=recv_sem.at[0],
        device_id=(gx, gy), device_id_type=MESH,
    ).wait_send()
    sums_in[:, 0:1, :] = sums[:, pl.ds(me, 1), :]
    landed = sums_in.at[:, pl.ds(1, devices - 1), :]
    pltpu.make_async_remote_copy(
        src_ref=landed, dst_ref=landed, send_sem=sums_send, recv_sem=sums_recv,
        device_id=(gx, gy), device_id_type=MESH,
    ).wait()
    for c in range(3):
        here = jnp.sum(sums_in[c], axis=0, keepdims=True)
        force[:, c * 128 : (c + 1) * 128] = here * (1.0 / 256.0) ** 0.5


def finish_kernel(vel, st, force, vel_out, st_out, force_out, sems):
    copies = [
        pltpu.make_async_copy(vel, vel_out, sems.at[0]),
        pltpu.make_async_copy(st.at[pl.ds(0, 3)], st_out.at[pl.ds(0, 3)], sems.at[1]),
        pltpu.make_async_copy(st.at[pl.ds(3, 3)], st_out.at[pl.ds(3, 3)], sems.at[2]),
    ]
    for copy in copies:
        copy.start()
    force_out[...] = force[...]
    for copy in copies:
        copy.wait()


def on_device(
    velocity,
    stress,
    region_id,
    buoyancy,
    lame_lambda,
    shear_mu,
    shell_rows,
    shell_target,
    shell_cell,
    pile_pier,
    pile_cell,
    pier_owner,
):
    vmem = pl.BlockSpec(memory_space=pltpu.VMEM)
    anywhere = pl.BlockSpec(memory_space=pl.ANY)
    in_hbm = pl.BlockSpec(memory_space=pltpu.HBM)
    dma = pltpu.SemaphoreType.DMA
    operands = (
        shell_target.reshape(1, 256),
        shell_cell.reshape(1, 256),
        buoyancy,
        lame_lambda,
        shear_mu,
        jnp.transpose(shell_rows, (1, 0, 2)),
        velocity,
        stress,
        region_id,
        pile_cell.reshape(256),
        pile_pier.reshape(1, 256),
        pier_owner.reshape(1, 128),
    )
    operands = [pltpu.with_memory_space_constraint(x, pltpu.HBM) for x in operands]
    fields = pltpu.VMEM((32, 64, 128), F32)
    edge_row = pltpu.VMEM((3, 32, 1, 128), F32)
    edge_plane = pltpu.VMEM((3, 64, 128), F32)
    table = pltpu.SMEM((16,), F32)
    vel, st, force = pl.pallas_call(
        wave_kernel,
        out_shape=(
            pltpu.VMEM((3, 32, 64, 128), F32), pltpu.VMEM((6, 32, 64, 128), F32), pltpu.VMEM((1, 384), F32)
        ),
        in_specs=[in_hbm] * len(operands),
        out_specs=(vmem, vmem, vmem),
        scratch_shapes=[
            pltpu.VMEM((1, 256), jnp.int32),
            pltpu.VMEM((1, 256), jnp.int32),
            table,
            table,
            table,
            pltpu.VMEM((9, 256, 128), F32),
            pltpu.VMEM((32, 64, 128), jnp.int32),
            fields,
            fields,
            fields,
            pltpu.SMEM((256,), jnp.int32),
            pltpu.VMEM((256,), jnp.int32),
            pltpu.VMEM((1, 256), jnp.int32),
            pltpu.VMEM((1, 128), jnp.int32),
            pltpu.VMEM((3, 256, 128), F32),
            pltpu.VMEM((512, 384), BF16),
            pltpu.VMEM((3, 128, 128), F32),
            pltpu.VMEM((3, 128, 128), F32),
            pltpu.VMEM((512, 1152), BF16),
            pltpu.VMEM((37, 128, 128), F32),
            pltpu.VMEM((37, 128, 128), F32),
            pltpu.VMEM((256, 1152), BF16),
            edge_plane,
            edge_row,
            edge_plane,
            edge_row,
            edge_row,
            edge_plane,
            edge_row,
            dma((13,)),
            dma,
            dma,
            dma((GROUPS,)),
            dma((8,)),
            dma((8,)),
            dma,
            dma,
        ],
        compiler_params=pltpu.CompilerParams(
            collective_id=0, has_side_effects=True, vmem_limit_bytes=40 << 20
        ),
    )(*operands)
    return pl.pallas_call(
        finish_kernel,
        out_shape=(
            jax.ShapeDtypeStruct((3, 32, 64, 128), F32),
            jax.ShapeDtypeStruct((6, 32, 64, 128), F32),
            jax.ShapeDtypeStruct((1, 384), F32),
        ),
        in_specs=[vmem, vmem, vmem],
        out_specs=(anywhere, anywhere, vmem),
        scratch_shapes=[
            dma((3,)),
        ],
        compiler_params=pltpu.CompilerParams(vmem_limit_bytes=40 << 20),
    )(vel, st, force)


def solution(mesh):
    return jax.shard_map(
        on_device,
        mesh=mesh,
        in_specs=(
            P(None, "gx", "gy", None),
            P(None, "gx", "gy", None),
            P("gx", "gy", None),
            P(),
            P(),
            P(),
            P(("gx", "gy"), None, None),
            P(("gx", "gy"), None),
            P(("gx", "gy"), None),
            P(("gx", "gy"), None),
            P(("gx", "gy"), None),
            P(),
        ),
        out_specs=(P(None, "gx", "gy", None), P(None, "gx", "gy", None), P(("gx", "gy"), None)),
        check_vma=False,
    )
```

```python
import functools

import jax
import jax.numpy as jnp
from jax import lax
from jax.experimental import pallas as pl
from jax.experimental.pallas import tpu as pltpu
from jax.sharding import PartitionSpec as P

PML = 8
STEP = 0.25
DAMP = 0.3
SLOTS = 4
GROUPS = 4
UNROLL = 4
MESH = pl.DeviceIdType.MESH
LOGICAL = pl.DeviceIdType.LOGICAL
F32 = jnp.float32
BF16 = jnp.bfloat16


def iota(shape, dim):
    return lax.broadcasted_iota(jnp.int32, shape, dim)


def split_in_two(values):
    high = values.astype(BF16)
    return high, (values - high.astype(F32)).astype(BF16)


def absorb(distance):
    ramp = jnp.maximum(0.0, (PML - distance) / PML)
    return 1.0 - DAMP * ramp * ramp


def z_before(field):
    return jnp.where(iota(field.shape, 1) == 0, 0.0, pltpu.roll(field, 1, 1))


def z_after(field):
    size = field.shape[1]
    return jnp.where(iota(field.shape, 1) == size - 1, 0.0, pltpu.roll(field, size - 1, 1))


def y_before(field):
    return jnp.where(iota(field.shape, 0) == 0, 0.0, pltpu.roll(field, 1, 0))


def y_after(field):
    size = field.shape[0]
    return jnp.where(iota(field.shape, 0) == size - 1, 0.0, pltpu.roll(field, size - 1, 0))


def column_of(row):
    size = row.shape[1]
    square = iota((size, size), 0) == iota((size, size), 1)
    return jnp.sum(jnp.where(square, row.astype(F32), 0.0), axis=1, keepdims=True)


def lookup(region, table_ref):
    values = [table_ref[i] for i in range(16)]
    for bit in range(4):
        mask = (region & (1 << bit)) != 0
        values = [jnp.where(mask, values[2 * i + 1], values[2 * i]) for i in range(len(values) // 2)]
    return values[0]


def peer(step, gx, gy):
    x = lax.rem(gx + step, 4)
    y = lax.rem(lax.div(gy, 2) + lax.div(step, 4) + step, 4)
    z = lax.rem(lax.div(gx, 4) + 2 * lax.div(gy, 8) + lax.div(step, 16) + step, 4)
    core = lax.rem(gy + lax.div(step, 64) + step, 2)
    return lax.rem(z, 2) * 64 + x * 16 + lax.div(z, 2) * 8 + y * 2 + core


def wave_kernel(
    target_in, cell_in, table_b_in, table_l_in, table_m_in, rows_in, velocity_in, stress_in, region_in,
    pile_cell_in, pile_pier_in, owner_in,
    vel, st, force,
    target, cell, table_b, table_l, table_m, rows, region, hb, hl, hm,
    pile_at, pile_cell, pile_pier, owner, traction, response, sums, sums_in,
    parts, outgoing, arrived, group, x_send, y_send, x_halo, y_halo, v_send, vx_halo, vy_halo,
    load_sem, own_sem, send_sem, recv_sem, halo_send, halo_recv, sums_send, sums_recv, on_edge, change,
):
    gx, gy = lax.axis_index("gx"), lax.axis_index("gy")
    count_x, count_y = 8, 16
    devices = count_x * count_y
    me = gx * count_y + gy
    loads = [
        pltpu.make_async_copy(source, landing, load_sem.at[i])
        for i, (source, landing) in enumerate((
            (target_in, target), (cell_in, cell), (rows_in, rows),
            (table_b_in, table_b), (table_l_in, table_l), (table_m_in, table_m), (region_in, region),
            (velocity_in, vel), (stress_in, st), (pile_cell_in, pile_at), (pile_cell_in, pile_cell),
            (pile_pier_in, pile_pier), (owner_in, owner),
        ))
    ]
    for load in loads:
        load.start()

    barrier = pltpu.get_barrier_semaphore()

    def greet(step, _):
        pl.semaphore_signal(
            barrier, inc=1, device_id=lax.rem(me + step, devices), device_id_type=LOGICAL
        )
        return 0

    lax.fori_loop(1, devices, greet, 0, unroll=8)
    for load in loads[:3]:
        load.wait()

    target_row = target[...]
    count = target_row.shape[1]
    target_col = column_of(target_row).astype(jnp.int32)
    same = (target_col == target_row) & (iota((count, count), 0) < iota((count, count), 1))
    rank_row = jnp.sum(jnp.where(same, 1.0, 0.0), axis=0, keepdims=True)
    cell_row = cell[...].astype(F32)
    for f in range(9):
        high, low = split_in_two(rows[f])
        parts[0:count, f * 128 : (f + 1) * 128] = high
        parts[count : 2 * count, f * 128 : (f + 1) * 128] = low
    named = target_row == iota((devices, count), 0)
    cells_out = jnp.zeros((devices, 128), F32)
    lane_slot = iota((devices, 128), 1) // 32
    for k in range(SLOTS):
        mine = named & (rank_row == float(k))
        pick = jnp.where(mine, 1.0, 0.0).astype(BF16)
        pick = jnp.concatenate([pick, pick], axis=1)
        cell_col = jnp.sum(jnp.where(mine, cell_row, 0.0), axis=1, keepdims=True)
        cells_out = jnp.where(lane_slot == k, cell_col, cells_out)
        for first in range(0, 9, 2):
            width = min(2, 9 - first)
            packed = jnp.dot(
                pick, parts[:, first * 128 : (first + width) * 128], preferred_element_type=F32
            )
            for f in range(width):
                outgoing[(first + f) * SLOTS + k] = packed[:, f * 128 : (f + 1) * 128]
    outgoing[9 * SLOTS] = cells_out

    pl.semaphore_wait(barrier, devices - 1)
    per_group = devices // GROUPS

    def send(step, _):
        to = peer(step, gx, gy)
        pltpu.make_async_remote_copy(
            src_ref=outgoing.at[:, to, :],
            dst_ref=arrived.at[:, step, :],
            send_sem=send_sem,
            recv_sem=recv_sem.at[lax.div(step, per_group)],
            device_id=to,
            device_id_type=LOGICAL,
        ).start()
        return 0

    lax.fori_loop(1, devices, send, 0, unroll=8)
    own = pltpu.make_async_copy(outgoing.at[:, me, :], arrived.at[:, 0, :], own_sem)
    own.start()

    for load in loads[3:]:
        load.wait()

    def materials(x, _):
        here = region[x]
        hb[x] = STEP * lookup(here, table_b)
        hl[x] = STEP * lookup(here, table_l)
        hm[x] = STEP * lookup(here, table_m)
        return 0

    lax.fori_loop(0, 32, materials, 0)
    at = column_of(pile_cell[...].reshape(1, 256)).astype(jnp.int32)
    pile_x, pile_y = gx * 32 + at // 64, gy * 64 + at % 64
    plane = absorb(jnp.minimum(pile_x, 255 - pile_x).astype(F32))
    plane = plane * absorb(jnp.minimum(pile_y, 1023 - pile_y).astype(F32))
    pile_factor = plane * absorb((127 - iota((256, 128), 1)).astype(F32))
    owner_col = column_of(owner[...])
    named = pile_pier[...] == iota((devices, 256), 0)
    slot_row = jnp.sum(jnp.where(named, owner_col, 0.0), axis=0, keepdims=True).astype(jnp.int32)
    owned = jnp.where(slot_row == iota((devices, 256), 0), 1.0, 0.0).astype(BF16)
    owned = jnp.concatenate([owned, owned], axis=1)
    lane = iota((1, 256), 1)
    edge_of = jnp.where(lane < 64, lane, lane + 31 * 64 - 64)
    edge_of = jnp.where(lane >= 128, (lane - 128) * 64, edge_of)
    edge_of = jnp.where(lane >= 160, (lane - 160) * 64 + 63, edge_of)
    edge_of = jnp.where(lane >= 192, -1, edge_of)
    on_edge[...] = jnp.where(at == edge_of, 1.0, 0.0).astype(BF16)
    change[...] = jnp.zeros(change.shape, BF16)
    own.wait()

    def gather_group(first):
        for f in range(9):
            for k in range(SLOTS):
                high, low = split_in_two(arrived[f * SLOTS + k, pl.ds(first, 32), :])
                group[k * 32 : (k + 1) * 32, f * 128 : (f + 1) * 128] = high
                group[128 + k * 32 : 128 + (k + 1) * 32, f * 128 : (f + 1) * 128] = low
        names = arrived[9 * SLOTS, pl.ds(first, 32), :]
        mine = iota((32, 128), 1) % 32 == iota((32, 128), 0)
        names = jnp.sum(jnp.where(mine, names, 0.0), axis=0, keepdims=True).astype(jnp.int32)
        return jnp.concatenate([names, names], axis=1)

    def add_group(names):
        def add_block(block, _):
            pick = jnp.where(iota((256, 256), 0) + block * 256 == names, 1.0, 0.0).astype(BF16)
            for first in range(0, 9, 2):
                width = min(2, 9 - first)
                added = jnp.dot(
                    pick, group[:, first * 128 : (first + width) * 128], preferred_element_type=F32
                )
                for f in range(width):
                    piece = added[:, f * 128 : (f + 1) * 128].reshape(4, 64, 128)
                    if first + f < 3:
                        vel[first + f, pl.ds(block * 4, 4)] += piece
                    else:
                        st[first + f - 3, pl.ds(block * 4, 4)] += piece
            return 0

        lax.fori_loop(0, 8, add_block, 0, unroll=UNROLL)

    for g in range(GROUPS):
        low = 1 if g == 0 else 0
        landed = arrived.at[:, pl.ds(g * per_group + low, per_group - low), :]
        pltpu.make_async_remote_copy(
            src_ref=landed, dst_ref=landed, send_sem=send_sem, recv_sem=recv_sem.at[g],
            device_id=(gx, gy), device_id_type=MESH,
        ).wait_recv()
        names = gather_group(g * per_group)
        if g < GROUPS - 1:
            add_group(names)

    x_after_dev = ((gx + 1) % count_x, gy)
    x_before_dev = ((gx + count_x - 1) % count_x, gy)
    y_after_dev = (gx, (gy + 1) % count_y)
    y_before_dev = (gx, (gy + count_y - 1) % count_y)
    has_x_before, has_x_after = gx > 0, gx < count_x - 1
    has_y_before, has_y_after = gy > 0, gy < count_y - 1

    def halo_copy(number, source, landing, device):
        return pltpu.make_async_remote_copy(
            src_ref=source, dst_ref=landing, send_sem=halo_send.at[number],
            recv_sem=halo_recv.at[number], device_id=device, device_id_type=MESH,
        )

    row = iota((192, 1), 0)
    column = jnp.where(row < 64, row, row + 31 * 64 - 64)
    column = jnp.where(row >= 128, (row - 128) * 64 + 63, column)
    column = jnp.where(row >= 160, (row - 160) * 64, column)
    pick = jnp.where(column == names, 1.0, 0.0).astype(BF16)
    edge = jnp.dot(pick, group[:, 384:1152], preferred_element_type=F32)
    x_send[0] = st[0, 0] + edge[0:64, 0:128]
    x_send[1] = st[3, 31] + edge[64:128, 384:512]
    x_send[2] = st[4, 31] + edge[64:128, 512:640]
    y_send[0] = st[3, :, 63:64, :] + edge[128:160, 384:512].reshape(32, 1, 128)
    y_send[1] = st[5, :, 63:64, :] + edge[128:160, 640:768].reshape(32, 1, 128)
    y_send[2] = st[1, :, 0:1, :] + edge[160:192, 128:256].reshape(32, 1, 128)
    stress_copies = [
        halo_copy(0, x_send.at[0], x_halo.at[0], x_before_dev),
        halo_copy(1, x_send.at[pl.ds(1, 2)], x_halo.at[pl.ds(1, 2)], x_after_dev),
        halo_copy(2, y_send.at[pl.ds(0, 2)], y_halo.at[pl.ds(0, 2)], y_after_dev),
        halo_copy(3, y_send.at[2], y_halo.at[2], y_before_dev),
    ]
    for copy in stress_copies:
        copy.start()
    add_group(names)

    def move_velocity(x, xx_after, xy_before, xz_before):
        xx, yy, zz, xy, xz, yz = [st[f, x] for f in range(6)]
        scaled = hb[x]
        vel[0, x] += scaled * ((xx_after - xx) + (xy - y_before(xy)) + (xz - z_before(xz)))
        vel[1, x] += scaled * ((xy - xy_before) + (y_after(yy) - yy) + (yz - z_before(yz)))
        vel[2, x] += scaled * ((xz - xz_before) + (yz - y_before(yz)) + (z_after(zz) - zz))

    def inner_velocity(x, _):
        move_velocity(x, st[0, x + 1], st[3, x - 1], st[4, x - 1])
        return 0

    lax.fori_loop(1, 31, inner_velocity, 0, unroll=2)
    for copy in stress_copies:
        copy.wait()
    move_velocity(
        0, st[0, 1], jnp.where(has_x_before, x_halo[1], 0.0), jnp.where(has_x_before, x_halo[2], 0.0)
    )
    move_velocity(31, jnp.where(has_x_after, x_halo[0], 0.0), st[3, 30], st[4, 30])
    top, bottom = hb[:, 0:1, :], hb[:, 63:64, :]
    vel[0, :, 0:1, :] -= top * jnp.where(has_y_before, y_halo[0], 0.0)
    vel[2, :, 0:1, :] -= top * jnp.where(has_y_before, y_halo[1], 0.0)
    vel[1, :, 63:64, :] += bottom * jnp.where(has_y_after, y_halo[2], 0.0)

    v_send[0] = vel[1, :, 63:64, :]
    v_send[1] = vel[0, :, 0:1, :]
    v_send[2] = vel[2, :, 0:1, :]
    velocity_copies = [
        halo_copy(4, vel.at[0, 31], vx_halo.at[0], x_after_dev),
        halo_copy(5, vel.at[pl.ds(1, 2), 0], vx_halo.at[pl.ds(1, 2)], x_before_dev),
        halo_copy(6, v_send.at[0], vy_halo.at[0], y_after_dev),
        halo_copy(7, v_send.at[pl.ds(1, 2)], vy_halo.at[pl.ds(1, 2)], y_before_dev),
    ]
    for copy in velocity_copies:
        copy.start()

    def move_pulled(x, vx_before, vz_after):
        vx, vy, vz = [vel[c, x] for c in range(3)]
        first, shear = hl[x], hm[x]
        strain_z = vz - z_before(vz)
        spread = first * ((vx - vx_before) + (vy - y_before(vy)) + strain_z)
        st[2, x] += spread + 2.0 * shear * strain_z
        st[4, x] += shear * ((vz_after - vz) + (z_after(vx) - vx))
        st[5, x] += shear * ((y_after(vz) - vz) + (z_after(vy) - vy))

    def inner_pulled(x, _):
        move_pulled(x, vel[0, x - 1], vel[2, x + 1])
        return 0

    nothing = jnp.zeros((64, 128), F32)
    move_pulled(0, nothing, vel[2, 1])
    lax.fori_loop(1, 31, inner_pulled, 0, unroll=2)
    move_pulled(31, vel[0, 30], nothing)

    def fetch(p, _):
        at = pile_at[p]
        x, y = lax.div(at, 64), lax.rem(at, 64)
        for c, f in enumerate((4, 5, 2)):
            traction[c, pl.ds(p, 1), :] = st[f, x, pl.ds(y, 1), :]
        return 0

    lax.fori_loop(0, 256, fetch, 0, unroll=8)
    for copy in velocity_copies:
        copy.wait()
    vx_edge = jnp.where(has_x_before, vx_halo[0], 0.0)
    vy_edge = jnp.where(has_y_before, vy_halo[0], 0.0)
    vz_edge = jnp.where(has_y_after, vy_halo[2], 0.0)
    zz_x = -hl[0] * vx_edge
    xz_x = hm[31] * jnp.where(has_x_after, vx_halo[2], 0.0)
    zz_y = -hl[:, 0:1, :] * vy_edge
    yz_y = hm[:, 63:64, :] * vz_edge
    for first, count, c, part in (
        (0, 64, 2, zz_x), (64, 64, 0, xz_x), (128, 32, 2, zz_y.reshape(32, 128)), (160, 32, 1, yz_y.reshape(32, 128))
    ):
        high, low = split_in_two(part)
        change[first : first + count, c * 128 : (c + 1) * 128] = high
        change[256 + first : 256 + first + count, c * 128 : (c + 1) * 128] = low
    pick = jnp.concatenate([on_edge[...], on_edge[...]], axis=1)
    changes = jnp.dot(pick, change[...], preferred_element_type=F32)
    for c in range(3):
        pulled = traction[c] + changes[:, c * 128 : (c + 1) * 128]
        high, low = split_in_two(jnp.tanh(pulled * pile_factor))
        response[0:256, c * 128 : (c + 1) * 128] = high
        response[256:512, c * 128 : (c + 1) * 128] = low
    total = jnp.dot(owned, response[...], preferred_element_type=F32)
    for c in range(3):
        sums[c] = total[:, c * 128 : (c + 1) * 128]

    def send_sum(step, _):
        to = lax.rem(me + step, devices)
        pltpu.make_async_remote_copy(
            src_ref=sums.at[:, to, :], dst_ref=sums_in.at[:, step, :],
            send_sem=sums_send, recv_sem=sums_recv, device_id=to, device_id_type=LOGICAL,
        ).start()
        return 0

    lax.fori_loop(1, devices, send_sum, 0, unroll=8)
    st[2, 0] += zz_x
    st[4, 31] += xz_x
    st[2, :, 0:1, :] += zz_y
    st[5, :, 63:64, :] += yz_y

    def move_rest(x, vx_before, vy_after):
        vx, vy, vz = [vel[c, x] for c in range(3)]
        first, shear = hl[x], hm[x]
        row = iota(vx.shape, 0)
        vy_before = jnp.where(row == 0, jnp.where(has_y_before, vy_halo[0, x], 0.0), pltpu.roll(vy, 1, 0))
        vx_after = jnp.where(row == 63, jnp.where(has_y_after, vy_halo[1, x], 0.0), pltpu.roll(vx, 63, 0))
        strain_x, strain_y, strain_z = vx - vx_before, vy - vy_before, vz - z_before(vz)
        spread = first * (strain_x + strain_y + strain_z)
        st[0, x] += spread + 2.0 * shear * strain_x
        st[1, x] += spread + 2.0 * shear * strain_y
        st[3, x] += shear * ((vy_after - vy) + (vx_after - vx))

    def inner_rest(x, _):
        move_rest(x, vel[0, x - 1], vel[1, x + 1])
        return 0

    move_rest(0, vx_edge, vel[1, 1])
    lax.fori_loop(1, 31, inner_rest, 0, unroll=2)
    move_rest(31, vel[0, 30], jnp.where(has_x_after, vx_halo[1], 0.0))

    y_index = gy * 64 + iota((64, 128), 0)
    along_y = absorb(jnp.minimum(y_index, 1023 - y_index).astype(F32))
    factor_yz = along_y * absorb((127 - iota((64, 128), 1)).astype(F32))

    def damp(x, _):
        x_index = gx * 32 + x
        far = jnp.broadcast_to(jnp.minimum(x_index, 255 - x_index), (64, 128)).astype(F32)
        factor = absorb(far) * factor_yz
        for c in range(3):
            vel[c, x] *= factor
        for f in range(6):
            st[f, x] *= factor
        return 0

    lax.fori_loop(0, 32, damp, 0)
    sent = outgoing.at[:, pl.ds(0, devices - 1), :]
    pltpu.make_async_remote_copy(
        src_ref=sent, dst_ref=sent, send_sem=send_sem, recv_sem=recv_sem.at[0],
        device_id=(gx, gy), device_id_type=MESH,
    ).wait_send()
    sums_in[:, 0:1, :] = sums[:, pl.ds(me, 1), :]
    landed = sums_in.at[:, pl.ds(1, devices - 1), :]
    pltpu.make_async_remote_copy(
        src_ref=landed, dst_ref=landed, send_sem=sums_send, recv_sem=sums_recv,
        device_id=(gx, gy), device_id_type=MESH,
    ).wait()
    for c in range(3):
        here = jnp.sum(sums_in[c], axis=0, keepdims=True)
        force[:, c * 128 : (c + 1) * 128] = here * (1.0 / 256.0) ** 0.5


def finish_kernel(vel, st, force, vel_out, st_out, force_out, sems):
    copies = [
        pltpu.make_async_copy(vel, vel_out, sems.at[0]),
        pltpu.make_async_copy(st.at[pl.ds(0, 3)], st_out.at[pl.ds(0, 3)], sems.at[1]),
        pltpu.make_async_copy(st.at[pl.ds(3, 3)], st_out.at[pl.ds(3, 3)], sems.at[2]),
    ]
    for copy in copies:
        copy.start()
    force_out[...] = force[...]
    for copy in copies:
        copy.wait()


def on_device(
    velocity,
    stress,
    region_id,
    buoyancy,
    lame_lambda,
    shear_mu,
    shell_rows,
    shell_target,
    shell_cell,
    pile_pier,
    pile_cell,
    pier_owner,
):
    vmem = pl.BlockSpec(memory_space=pltpu.VMEM)
    anywhere = pl.BlockSpec(memory_space=pl.ANY)
    in_hbm = pl.BlockSpec(memory_space=pltpu.HBM)
    dma = pltpu.SemaphoreType.DMA
    operands = (
        shell_target.reshape(1, 256),
        shell_cell.reshape(1, 256),
        buoyancy,
        lame_lambda,
        shear_mu,
        jnp.transpose(shell_rows, (1, 0, 2)),
        velocity,
        stress,
        region_id,
        pile_cell.reshape(256),
        pile_pier.reshape(1, 256),
        pier_owner.reshape(1, 128),
    )
    operands = [pltpu.with_memory_space_constraint(x, pltpu.HBM) for x in operands]
    fields = pltpu.VMEM((32, 64, 128), F32)
    edge_row = pltpu.VMEM((3, 32, 1, 128), F32)
    edge_plane = pltpu.VMEM((3, 64, 128), F32)
    table = pltpu.SMEM((16,), F32)
    vel, st, force = pl.pallas_call(
        wave_kernel,
        out_shape=(
            pltpu.VMEM((3, 32, 64, 128), F32), pltpu.VMEM((6, 32, 64, 128), F32), pltpu.VMEM((1, 384), F32)
        ),
        in_specs=[in_hbm] * len(operands),
        out_specs=(vmem, vmem, vmem),
        scratch_shapes=[
            pltpu.VMEM((1, 256), jnp.int32),
            pltpu.VMEM((1, 256), jnp.int32),
            table,
            table,
            table,
            pltpu.VMEM((9, 256, 128), F32),
            pltpu.VMEM((32, 64, 128), jnp.int32),
            fields,
            fields,
            fields,
            pltpu.SMEM((256,), jnp.int32),
            pltpu.VMEM((256,), jnp.int32),
            pltpu.VMEM((1, 256), jnp.int32),
            pltpu.VMEM((1, 128), jnp.int32),
            pltpu.VMEM((3, 256, 128), F32),
            pltpu.VMEM((512, 384), BF16),
            pltpu.VMEM((3, 128, 128), F32),
            pltpu.VMEM((3, 128, 128), F32),
            pltpu.VMEM((512, 1152), BF16),
            pltpu.VMEM((37, 128, 128), F32),
            pltpu.VMEM((37, 128, 128), F32),
            pltpu.VMEM((256, 1152), BF16),
            edge_plane,
            edge_row,
            edge_plane,
            edge_row,
            edge_row,
            edge_plane,
            edge_row,
            dma((13,)),
            dma,
            dma,
            dma((GROUPS,)),
            dma((8,)),
            dma((8,)),
            dma,
            dma,
            pltpu.VMEM((256, 256), BF16),
            pltpu.VMEM((512, 384), BF16),
        ],
        compiler_params=pltpu.CompilerParams(
            collective_id=0, has_side_effects=True, vmem_limit_bytes=40 << 20
        ),
    )(*operands)
    return pl.pallas_call(
        finish_kernel,
        out_shape=(
            jax.ShapeDtypeStruct((3, 32, 64, 128), F32),
            jax.ShapeDtypeStruct((6, 32, 64, 128), F32),
            jax.ShapeDtypeStruct((1, 384), F32),
        ),
        in_specs=[vmem, vmem, vmem],
        out_specs=(anywhere, anywhere, vmem),
        scratch_shapes=[
            dma((3,)),
        ],
        compiler_params=pltpu.CompilerParams(vmem_limit_bytes=40 << 20),
    )(vel, st, force)


def solution(mesh):
    return jax.shard_map(
        on_device,
        mesh=mesh,
        in_specs=(
            P(None, "gx", "gy", None),
            P(None, "gx", "gy", None),
            P("gx", "gy", None),
            P(),
            P(),
            P(),
            P(("gx", "gy"), None, None),
            P(("gx", "gy"), None),
            P(("gx", "gy"), None),
            P(("gx", "gy"), None),
            P(("gx", "gy"), None),
            P(),
        ),
        out_specs=(P(None, "gx", "gy", None), P(None, "gx", "gy", None), P(("gx", "gy"), None)),
        check_vma=False,
    )
```

```python
import functools

import jax
import jax.numpy as jnp
from jax import lax
from jax.experimental import pallas as pl
from jax.experimental.pallas import tpu as pltpu
from jax.sharding import PartitionSpec as P

PML = 8
STEP = 0.25
DAMP = 0.3
SLOTS = 4
GROUPS = 4
UNROLL = 4
MESH = pl.DeviceIdType.MESH
LOGICAL = pl.DeviceIdType.LOGICAL
F32 = jnp.float32
BF16 = jnp.bfloat16


def iota(shape, dim):
    return lax.broadcasted_iota(jnp.int32, shape, dim)


def split_in_two(values):
    high = values.astype(BF16)
    return high, (values - high.astype(F32)).astype(BF16)


def absorb(distance):
    ramp = jnp.maximum(0.0, (PML - distance) / PML)
    return 1.0 - DAMP * ramp * ramp


def z_before(field):
    return jnp.where(iota(field.shape, 1) == 0, 0.0, pltpu.roll(field, 1, 1))


def z_after(field):
    size = field.shape[1]
    return jnp.where(iota(field.shape, 1) == size - 1, 0.0, pltpu.roll(field, size - 1, 1))


def y_before(field):
    return jnp.where(iota(field.shape, 0) == 0, 0.0, pltpu.roll(field, 1, 0))


def y_after(field):
    size = field.shape[0]
    return jnp.where(iota(field.shape, 0) == size - 1, 0.0, pltpu.roll(field, size - 1, 0))


def column_of(row):
    size = row.shape[1]
    square = iota((size, size), 0) == iota((size, size), 1)
    return jnp.sum(jnp.where(square, row.astype(F32), 0.0), axis=1, keepdims=True)


def lookup(region, table_ref):
    values = [table_ref[i] for i in range(16)]
    for bit in range(4):
        mask = (region & (1 << bit)) != 0
        values = [jnp.where(mask, values[2 * i + 1], values[2 * i]) for i in range(len(values) // 2)]
    return values[0]


def peer(step, gx, gy):
    x = lax.rem(gx + step, 4)
    y = lax.rem(lax.div(gy, 2) + lax.div(step, 4) + step, 4)
    z = lax.rem(lax.div(gx, 4) + 2 * lax.div(gy, 8) + lax.div(step, 16) + step, 4)
    core = lax.rem(gy + lax.div(step, 64) + step, 2)
    return lax.rem(z, 2) * 64 + x * 16 + lax.div(z, 2) * 8 + y * 2 + core


def wave_kernel(
    target_in, cell_in, table_b_in, table_l_in, table_m_in, rows_in, velocity_in, stress_in, region_in,
    pile_cell_in, pile_pier_in, owner_in,
    vel, st, force,
    target, cell, table_b, table_l, table_m, rows, region, hb, hl, hm,
    pile_at, pile_cell, pile_pier, owner, traction, response, sums, sums_in,
    parts, outgoing, arrived, group, x_send, y_send, x_halo, y_halo, v_send, vx_halo, vy_halo,
    load_sem, own_sem, send_sem, recv_sem, halo_send, halo_recv, sums_send, sums_recv, on_edge, change,
):
    gx, gy = lax.axis_index("gx"), lax.axis_index("gy")
    count_x, count_y = 8, 16
    devices = count_x * count_y
    me = gx * count_y + gy
    loads = [
        pltpu.make_async_copy(source, landing, load_sem.at[i])
        for i, (source, landing) in enumerate((
            (target_in, target), (cell_in, cell), (rows_in, rows),
            (table_b_in, table_b), (table_l_in, table_l), (table_m_in, table_m), (region_in, region),
            (velocity_in, vel), (stress_in, st), (pile_cell_in, pile_at), (pile_cell_in, pile_cell),
            (pile_pier_in, pile_pier), (owner_in, owner),
        ))
    ]
    for load in loads:
        load.start()

    barrier = pltpu.get_barrier_semaphore()

    def greet(step, _):
        pl.semaphore_signal(
            barrier, inc=1, device_id=lax.rem(me + step, devices), device_id_type=LOGICAL
        )
        return 0

    lax.fori_loop(1, devices, greet, 0, unroll=8)
    for load in loads[:3]:
        load.wait()

    target_row = target[...]
    count = target_row.shape[1]
    target_col = column_of(target_row).astype(jnp.int32)
    same = (target_col == target_row) & (iota((count, count), 0) < iota((count, count), 1))
    rank_row = jnp.sum(jnp.where(same, 1.0, 0.0), axis=0, keepdims=True)
    cell_row = cell[...].astype(F32)
    for f in range(9):
        high, low = split_in_two(rows[f])
        parts[0:count, f * 128 : (f + 1) * 128] = high
        parts[count : 2 * count, f * 128 : (f + 1) * 128] = low
    named = target_row == iota((devices, count), 0)
    cells_out = jnp.zeros((devices, 128), F32)
    lane_slot = iota((devices, 128), 1) // 32
    for k in range(SLOTS):
        mine = named & (rank_row == float(k))
        pick = jnp.where(mine, 1.0, 0.0).astype(BF16)
        pick = jnp.concatenate([pick, pick], axis=1)
        cell_col = jnp.sum(jnp.where(mine, cell_row, 0.0), axis=1, keepdims=True)
        cells_out = jnp.where(lane_slot == k, cell_col, cells_out)
        for first in range(0, 9, 2):
            width = min(2, 9 - first)
            packed = jnp.dot(
                pick, parts[:, first * 128 : (first + width) * 128], preferred_element_type=F32
            )
            for f in range(width):
                outgoing[(first + f) * SLOTS + k] = packed[:, f * 128 : (f + 1) * 128]
    outgoing[9 * SLOTS] = cells_out

    pl.semaphore_wait(barrier, devices - 1)
    per_group = devices // GROUPS

    def send(step, _):
        to = peer(step, gx, gy)
        pltpu.make_async_remote_copy(
            src_ref=outgoing.at[:, to, :],
            dst_ref=arrived.at[:, step, :],
            send_sem=send_sem,
            recv_sem=recv_sem.at[lax.div(step, per_group)],
            device_id=to,
            device_id_type=LOGICAL,
        ).start()
        return 0

    lax.fori_loop(1, devices, send, 0, unroll=8)
    own = pltpu.make_async_copy(outgoing.at[:, me, :], arrived.at[:, 0, :], own_sem)
    own.start()

    for load in loads[3:]:
        load.wait()

    def materials(x, _):
        here = region[x]
        hb[x] = STEP * lookup(here, table_b)
        hl[x] = STEP * lookup(here, table_l)
        hm[x] = STEP * lookup(here, table_m)
        return 0

    lax.fori_loop(0, 32, materials, 0)
    at = column_of(pile_cell[...].reshape(1, 256)).astype(jnp.int32)
    pile_x, pile_y = gx * 32 + at // 64, gy * 64 + at % 64
    plane = absorb(jnp.minimum(pile_x, 255 - pile_x).astype(F32))
    plane = plane * absorb(jnp.minimum(pile_y, 1023 - pile_y).astype(F32))
    pile_factor = plane * absorb((127 - iota((256, 128), 1)).astype(F32))
    owner_col = column_of(owner[...])
    named = pile_pier[...] == iota((devices, 256), 0)
    slot_row = jnp.sum(jnp.where(named, owner_col, 0.0), axis=0, keepdims=True).astype(jnp.int32)
    owned = jnp.where(slot_row == iota((devices, 256), 0), 1.0, 0.0).astype(BF16)
    owned = jnp.concatenate([owned, owned], axis=1)
    lane = iota((1, 256), 1)
    edge_of = jnp.where(lane < 64, lane, lane + 31 * 64 - 64)
    edge_of = jnp.where(lane >= 128, (lane - 128) * 64, edge_of)
    edge_of = jnp.where(lane >= 160, (lane - 160) * 64 + 63, edge_of)
    edge_of = jnp.where(lane >= 192, -1, edge_of)
    on_edge[...] = jnp.where(at == edge_of, 1.0, 0.0).astype(BF16)
    change[...] = jnp.zeros(change.shape, BF16)
    own.wait()

    def gather_group(first):
        for f in range(9):
            for k in range(SLOTS):
                high, low = split_in_two(arrived[f * SLOTS + k, pl.ds(first, 32), :])
                group[k * 32 : (k + 1) * 32, f * 128 : (f + 1) * 128] = high
                group[128 + k * 32 : 128 + (k + 1) * 32, f * 128 : (f + 1) * 128] = low
        names = arrived[9 * SLOTS, pl.ds(first, 32), :]
        mine = iota((32, 128), 1) % 32 == iota((32, 128), 0)
        names = jnp.sum(jnp.where(mine, names, 0.0), axis=0, keepdims=True).astype(jnp.int32)
        return jnp.concatenate([names, names], axis=1)

    def add_group(names):
        def add_block(block, _):
            pick = jnp.where(iota((256, 256), 0) + block * 256 == names, 1.0, 0.0).astype(BF16)
            for first in range(0, 9, 2):
                width = min(2, 9 - first)
                added = jnp.dot(
                    pick, group[:, first * 128 : (first + width) * 128], preferred_element_type=F32
                )
                for f in range(width):
                    piece = added[:, f * 128 : (f + 1) * 128].reshape(4, 64, 128)
                    if first + f < 3:
                        vel[first + f, pl.ds(block * 4, 4)] += piece
                    else:
                        st[first + f - 3, pl.ds(block * 4, 4)] += piece
            return 0

        lax.fori_loop(0, 8, add_block, 0, unroll=UNROLL)

    for g in range(GROUPS):
        low = 1 if g == 0 else 0
        landed = arrived.at[:, pl.ds(g * per_group + low, per_group - low), :]
        pltpu.make_async_remote_copy(
            src_ref=landed, dst_ref=landed, send_sem=send_sem, recv_sem=recv_sem.at[g],
            device_id=(gx, gy), device_id_type=MESH,
        ).wait_recv()
        names = gather_group(g * per_group)
        if g < GROUPS - 1:
            add_group(names)

    x_after_dev = ((gx + 1) % count_x, gy)
    x_before_dev = ((gx + count_x - 1) % count_x, gy)
    y_after_dev = (gx, (gy + 1) % count_y)
    y_before_dev = (gx, (gy + count_y - 1) % count_y)
    has_x_before, has_x_after = gx > 0, gx < count_x - 1
    has_y_before, has_y_after = gy > 0, gy < count_y - 1

    def halo_copy(number, source, landing, device):
        return pltpu.make_async_remote_copy(
            src_ref=source, dst_ref=landing, send_sem=halo_send.at[number],
            recv_sem=halo_recv.at[number], device_id=device, device_id_type=MESH,
        )

    x_up, x_down = (has_x_after, has_x_before), (has_x_before, has_x_after)
    y_up, y_down = (has_y_after, has_y_before), (has_y_before, has_y_after)

    def start_halo(copies, ways):
        for copy, (sends, _) in zip(copies, ways):
            pl.when(sends)(copy.start)

    def wait_halo(copies, ways):
        for copy, (sends, receives) in zip(copies, ways):
            pl.when(sends)(copy.wait_send)
            pl.when(receives)(copy.wait_recv)

    row = iota((192, 1), 0)
    column = jnp.where(row < 64, row, row + 31 * 64 - 64)
    column = jnp.where(row >= 128, (row - 128) * 64 + 63, column)
    column = jnp.where(row >= 160, (row - 160) * 64, column)
    pick = jnp.where(column == names, 1.0, 0.0).astype(BF16)
    edge = jnp.dot(pick, group[:, 384:1152], preferred_element_type=F32)
    x_send[0] = st[0, 0] + edge[0:64, 0:128]
    x_send[1] = st[3, 31] + edge[64:128, 384:512]
    x_send[2] = st[4, 31] + edge[64:128, 512:640]
    y_send[0] = st[3, :, 63:64, :] + edge[128:160, 384:512].reshape(32, 1, 128)
    y_send[1] = st[5, :, 63:64, :] + edge[128:160, 640:768].reshape(32, 1, 128)
    y_send[2] = st[1, :, 0:1, :] + edge[160:192, 128:256].reshape(32, 1, 128)
    stress_copies = [
        halo_copy(0, x_send.at[0], x_halo.at[0], x_before_dev),
        halo_copy(1, x_send.at[pl.ds(1, 2)], x_halo.at[pl.ds(1, 2)], x_after_dev),
        halo_copy(2, y_send.at[pl.ds(0, 2)], y_halo.at[pl.ds(0, 2)], y_after_dev),
        halo_copy(3, y_send.at[2], y_halo.at[2], y_before_dev),
    ]
    stress_ways = (x_down, x_up, y_up, y_down)
    start_halo(stress_copies, stress_ways)
    add_group(names)

    def move_velocity(x, xx_after, xy_before, xz_before):
        xx, yy, zz, xy, xz, yz = [st[f, x] for f in range(6)]
        scaled = hb[x]
        vel[0, x] += scaled * ((xx_after - xx) + (xy - y_before(xy)) + (xz - z_before(xz)))
        vel[1, x] += scaled * ((xy - xy_before) + (y_after(yy) - yy) + (yz - z_before(yz)))
        vel[2, x] += scaled * ((xz - xz_before) + (yz - y_before(yz)) + (z_after(zz) - zz))

    def inner_velocity(x, _):
        move_velocity(x, st[0, x + 1], st[3, x - 1], st[4, x - 1])
        return 0

    lax.fori_loop(1, 31, inner_velocity, 0, unroll=2)
    wait_halo(stress_copies, stress_ways)
    move_velocity(
        0, st[0, 1], jnp.where(has_x_before, x_halo[1], 0.0), jnp.where(has_x_before, x_halo[2], 0.0)
    )
    move_velocity(31, jnp.where(has_x_after, x_halo[0], 0.0), st[3, 30], st[4, 30])
    top, bottom = hb[:, 0:1, :], hb[:, 63:64, :]
    vel[0, :, 0:1, :] -= top * jnp.where(has_y_before, y_halo[0], 0.0)
    vel[2, :, 0:1, :] -= top * jnp.where(has_y_before, y_halo[1], 0.0)
    vel[1, :, 63:64, :] += bottom * jnp.where(has_y_after, y_halo[2], 0.0)

    v_send[0] = vel[1, :, 63:64, :]
    v_send[1] = vel[0, :, 0:1, :]
    v_send[2] = vel[2, :, 0:1, :]
    velocity_copies = [
        halo_copy(4, vel.at[0, 31], vx_halo.at[0], x_after_dev),
        halo_copy(5, vel.at[pl.ds(1, 2), 0], vx_halo.at[pl.ds(1, 2)], x_before_dev),
        halo_copy(6, v_send.at[0], vy_halo.at[0], y_after_dev),
        halo_copy(7, v_send.at[pl.ds(1, 2)], vy_halo.at[pl.ds(1, 2)], y_before_dev),
    ]
    velocity_ways = (x_up, x_down, y_up, y_down)
    start_halo(velocity_copies, velocity_ways)

    def move_pulled(x, vx_before, vz_after):
        vx, vy, vz = [vel[c, x] for c in range(3)]
        first, shear = hl[x], hm[x]
        strain_z = vz - z_before(vz)
        spread = first * ((vx - vx_before) + (vy - y_before(vy)) + strain_z)
        st[2, x] += spread + 2.0 * shear * strain_z
        st[4, x] += shear * ((vz_after - vz) + (z_after(vx) - vx))
        st[5, x] += shear * ((y_after(vz) - vz) + (z_after(vy) - vy))

    def inner_pulled(x, _):
        move_pulled(x, vel[0, x - 1], vel[2, x + 1])
        return 0

    nothing = jnp.zeros((64, 128), F32)
    move_pulled(0, nothing, vel[2, 1])
    lax.fori_loop(1, 31, inner_pulled, 0, unroll=2)
    move_pulled(31, vel[0, 30], nothing)

    def fetch(p, _):
        at = pile_at[p]
        x, y = lax.div(at, 64), lax.rem(at, 64)
        for c, f in enumerate((4, 5, 2)):
            traction[c, pl.ds(p, 1), :] = st[f, x, pl.ds(y, 1), :]
        return 0

    lax.fori_loop(0, 256, fetch, 0, unroll=8)
    wait_halo(velocity_copies, velocity_ways)
    vx_edge = jnp.where(has_x_before, vx_halo[0], 0.0)
    vy_edge = jnp.where(has_y_before, vy_halo[0], 0.0)
    vz_edge = jnp.where(has_y_after, vy_halo[2], 0.0)
    zz_x = -hl[0] * vx_edge
    xz_x = hm[31] * jnp.where(has_x_after, vx_halo[2], 0.0)
    zz_y = -hl[:, 0:1, :] * vy_edge
    yz_y = hm[:, 63:64, :] * vz_edge
    for first, count, c, part in (
        (0, 64, 2, zz_x), (64, 64, 0, xz_x), (128, 32, 2, zz_y.reshape(32, 128)), (160, 32, 1, yz_y.reshape(32, 128))
    ):
        high, low = split_in_two(part)
        change[first : first + count, c * 128 : (c + 1) * 128] = high
        change[256 + first : 256 + first + count, c * 128 : (c + 1) * 128] = low
    pick = jnp.concatenate([on_edge[...], on_edge[...]], axis=1)
    changes = jnp.dot(pick, change[...], preferred_element_type=F32)
    for c in range(3):
        pulled = traction[c] + changes[:, c * 128 : (c + 1) * 128]
        high, low = split_in_two(jnp.tanh(pulled * pile_factor))
        response[0:256, c * 128 : (c + 1) * 128] = high
        response[256:512, c * 128 : (c + 1) * 128] = low
    total = jnp.dot(owned, response[...], preferred_element_type=F32)
    for c in range(3):
        sums[c] = total[:, c * 128 : (c + 1) * 128]

    def send_sum(step, _):
        to = lax.rem(me + step, devices)
        pltpu.make_async_remote_copy(
            src_ref=sums.at[:, to, :], dst_ref=sums_in.at[:, step, :],
            send_sem=sums_send, recv_sem=sums_recv, device_id=to, device_id_type=LOGICAL,
        ).start()
        return 0

    lax.fori_loop(1, devices, send_sum, 0, unroll=8)
    st[2, 0] += zz_x
    st[4, 31] += xz_x
    st[2, :, 0:1, :] += zz_y
    st[5, :, 63:64, :] += yz_y

    def move_rest(x, vx_before, vy_after):
        vx, vy, vz = [vel[c, x] for c in range(3)]
        first, shear = hl[x], hm[x]
        row = iota(vx.shape, 0)
        vy_before = jnp.where(row == 0, jnp.where(has_y_before, vy_halo[0, x], 0.0), pltpu.roll(vy, 1, 0))
        vx_after = jnp.where(row == 63, jnp.where(has_y_after, vy_halo[1, x], 0.0), pltpu.roll(vx, 63, 0))
        strain_x, strain_y, strain_z = vx - vx_before, vy - vy_before, vz - z_before(vz)
        spread = first * (strain_x + strain_y + strain_z)
        st[0, x] += spread + 2.0 * shear * strain_x
        st[1, x] += spread + 2.0 * shear * strain_y
        st[3, x] += shear * ((vy_after - vy) + (vx_after - vx))

    def inner_rest(x, _):
        move_rest(x, vel[0, x - 1], vel[1, x + 1])
        return 0

    move_rest(0, vx_edge, vel[1, 1])
    lax.fori_loop(1, 31, inner_rest, 0, unroll=2)
    move_rest(31, vel[0, 30], jnp.where(has_x_after, vx_halo[1], 0.0))

    y_index = gy * 64 + iota((64, 128), 0)
    along_y = absorb(jnp.minimum(y_index, 1023 - y_index).astype(F32))
    factor_yz = along_y * absorb((127 - iota((64, 128), 1)).astype(F32))

    def damp(x, _):
        x_index = gx * 32 + x
        far = jnp.broadcast_to(jnp.minimum(x_index, 255 - x_index), (64, 128)).astype(F32)
        factor = absorb(far) * factor_yz
        for c in range(3):
            vel[c, x] *= factor
        for f in range(6):
            st[f, x] *= factor
        return 0

    lax.fori_loop(0, 32, damp, 0)
    sent = outgoing.at[:, pl.ds(0, devices - 1), :]
    pltpu.make_async_remote_copy(
        src_ref=sent, dst_ref=sent, send_sem=send_sem, recv_sem=recv_sem.at[0],
        device_id=(gx, gy), device_id_type=MESH,
    ).wait_send()
    sums_in[:, 0:1, :] = sums[:, pl.ds(me, 1), :]
    landed = sums_in.at[:, pl.ds(1, devices - 1), :]
    pltpu.make_async_remote_copy(
        src_ref=landed, dst_ref=landed, send_sem=sums_send, recv_sem=sums_recv,
        device_id=(gx, gy), device_id_type=MESH,
    ).wait()
    for c in range(3):
        here = jnp.sum(sums_in[c], axis=0, keepdims=True)
        force[:, c * 128 : (c + 1) * 128] = here * (1.0 / 256.0) ** 0.5


def finish_kernel(vel, st, force, vel_out, st_out, force_out, sems):
    copies = [
        pltpu.make_async_copy(vel, vel_out, sems.at[0]),
        pltpu.make_async_copy(st.at[pl.ds(0, 3)], st_out.at[pl.ds(0, 3)], sems.at[1]),
        pltpu.make_async_copy(st.at[pl.ds(3, 3)], st_out.at[pl.ds(3, 3)], sems.at[2]),
    ]
    for copy in copies:
        copy.start()
    force_out[...] = force[...]
    for copy in copies:
        copy.wait()


def on_device(
    velocity,
    stress,
    region_id,
    buoyancy,
    lame_lambda,
    shear_mu,
    shell_rows,
    shell_target,
    shell_cell,
    pile_pier,
    pile_cell,
    pier_owner,
):
    vmem = pl.BlockSpec(memory_space=pltpu.VMEM)
    anywhere = pl.BlockSpec(memory_space=pl.ANY)
    in_hbm = pl.BlockSpec(memory_space=pltpu.HBM)
    dma = pltpu.SemaphoreType.DMA
    operands = (
        shell_target.reshape(1, 256),
        shell_cell.reshape(1, 256),
        buoyancy,
        lame_lambda,
        shear_mu,
        jnp.transpose(shell_rows, (1, 0, 2)),
        velocity,
        stress,
        region_id,
        pile_cell.reshape(256),
        pile_pier.reshape(1, 256),
        pier_owner.reshape(1, 128),
    )
    operands = [pltpu.with_memory_space_constraint(x, pltpu.HBM) for x in operands]
    fields = pltpu.VMEM((32, 64, 128), F32)
    edge_row = pltpu.VMEM((3, 32, 1, 128), F32)
    edge_plane = pltpu.VMEM((3, 64, 128), F32)
    table = pltpu.SMEM((16,), F32)
    vel, st, force = pl.pallas_call(
        wave_kernel,
        out_shape=(
            pltpu.VMEM((3, 32, 64, 128), F32), pltpu.VMEM((6, 32, 64, 128), F32), pltpu.VMEM((1, 384), F32)
        ),
        in_specs=[in_hbm] * len(operands),
        out_specs=(vmem, vmem, vmem),
        scratch_shapes=[
            pltpu.VMEM((1, 256), jnp.int32),
            pltpu.VMEM((1, 256), jnp.int32),
            table,
            table,
            table,
            pltpu.VMEM((9, 256, 128), F32),
            pltpu.VMEM((32, 64, 128), jnp.int32),
            fields,
            fields,
            fields,
            pltpu.SMEM((256,), jnp.int32),
            pltpu.VMEM((256,), jnp.int32),
            pltpu.VMEM((1, 256), jnp.int32),
            pltpu.VMEM((1, 128), jnp.int32),
            pltpu.VMEM((3, 256, 128), F32),
            pltpu.VMEM((512, 384), BF16),
            pltpu.VMEM((3, 128, 128), F32),
            pltpu.VMEM((3, 128, 128), F32),
            pltpu.VMEM((512, 1152), BF16),
            pltpu.VMEM((37, 128, 128), F32),
            pltpu.VMEM((37, 128, 128), F32),
            pltpu.VMEM((256, 1152), BF16),
            edge_plane,
            edge_row,
            edge_plane,
            edge_row,
            edge_row,
            edge_plane,
            edge_row,
            dma((13,)),
            dma,
            dma,
            dma((GROUPS,)),
            dma((8,)),
            dma((8,)),
            dma,
            dma,
            pltpu.VMEM((256, 256), BF16),
            pltpu.VMEM((512, 384), BF16),
        ],
        compiler_params=pltpu.CompilerParams(
            collective_id=0, has_side_effects=True, vmem_limit_bytes=40 << 20
        ),
    )(*operands)
    return pl.pallas_call(
        finish_kernel,
        out_shape=(
            jax.ShapeDtypeStruct((3, 32, 64, 128), F32),
            jax.ShapeDtypeStruct((6, 32, 64, 128), F32),
            jax.ShapeDtypeStruct((1, 384), F32),
        ),
        in_specs=[vmem, vmem, vmem],
        out_specs=(anywhere, anywhere, vmem),
        scratch_shapes=[
            dma((3,)),
        ],
        compiler_params=pltpu.CompilerParams(vmem_limit_bytes=40 << 20),
    )(vel, st, force)


def solution(mesh):
    return jax.shard_map(
        on_device,
        mesh=mesh,
        in_specs=(
            P(None, "gx", "gy", None),
            P(None, "gx", "gy", None),
            P("gx", "gy", None),
            P(),
            P(),
            P(),
            P(("gx", "gy"), None, None),
            P(("gx", "gy"), None),
            P(("gx", "gy"), None),
            P(("gx", "gy"), None),
            P(("gx", "gy"), None),
            P(),
        ),
        out_specs=(P(None, "gx", "gy", None), P(None, "gx", "gy", None), P(("gx", "gy"), None)),
        check_vma=False,
    )
```
